32 devices in a mesh: space: 16 (over z, x, core), chan: 2 (over y).
Axes of the slice: x: 2, y: 2, z: 4, core: 2. Of those that a mesh axis runs over, the one named last changes fastest.
Arguments:
- field: bfloat16 [256, 8, 2048], P('chan', None, 'space'), may hold values from -6 to 6
- first_weight: bfloat16 [256, 9, 256], P('chan'), may hold values from -0.125 to 0.125
- second_weight: bfloat16 [256, 9, 256], P('chan'), may hold values from -0.125 to 0.125
- cotangent: bfloat16 [256, 8, 2048], P('chan', None, 'space'), may hold values from -6 to 6
Outputs:
- field_grad: bfloat16 [256, 8, 2048], P('chan', None, 'space')
- first_grad: float32 [256, 9, 256], P('chan')
- second_grad: float32 [256, 9, 256], P('chan')
The draws below stay inside these ranges and needn't reach their ends.
All inputs are finite; a program needn't handle non-finite values.
Results may differ from the reference program's by a relative error of at most 0.0053.
Values may be sent and summed in bfloat16 or wider, within the bound.
No kernel may reach another device: no remote copies, remote signals or barrier semaphores. Data moves between devices by JAX's collectives and lax.ppermute only.
A program may use at most 64 MiB of HBM per device.

```python
import math
import jax
import jax.numpy as jnp

C = 256
ROWS = 8
COLS = 2048


def block_scale(key, dims, cuts, low, high):
    level = 1.0
    for position, parts in cuts:
        draws = jax.random.uniform(jax.random.fold_in(jax.random.fold_in(key, 6), position), (parts,), jnp.float32, low / len(cuts), high / len(cuts))
        level = level * jnp.repeat(jnp.exp(draws), dims[position] // parts).reshape((-1,) + (1,) * (len(dims) - 1 - position))
    return level


def bell_draw(stream_key, shape, scale, most, cuts=(), held_as=jnp.bfloat16):
    array = jax.random.normal(stream_key, shape, jnp.float32) * scale
    if len(cuts) > 0:
        array = block_scale(stream_key, shape, cuts, -0.22, 0.18) * array
    return jnp.clip(array, min=-most, max=most).astype(held_as)


def setup_inputs(seed: int = 0) -> dict:
    arg_keys = jax.random.split(jax.random.key(seed), 5)
    field = bell_draw(arg_keys[0], (C, ROWS, COLS), 1.0, 6.0, ((0, 2), (2, 16)))
    first_weight = bell_draw(arg_keys[1], (C, 9, C), (9 * C) ** -0.5, 0.125, ((0, 2),))
    second_weight = bell_draw(arg_keys[2], (C, 9, C), (9 * C) ** -0.5, 0.125, ((0, 2),))
    cotangent = bell_draw(arg_keys[3], (C, ROWS, COLS), 1.0, 6.0, ((0, 2), (2, 16)))
    return {"field": field, "first_weight": first_weight, "second_weight": second_weight, "cotangent": cotangent}


def wrap_cols(values, width):
    return jnp.concatenate([values[:, :, -width:], values, values[:, :, :width]], axis=2)

def pad_rows(values):
    return jnp.pad(values, ((0, 0), (1, 1), (0, 0)))

def conv_forward(padded, weight):
    height = padded.shape[1] - 2
    length = padded.shape[2] - 2
    total = jnp.zeros((weight.shape[0], height, length), jnp.float32)
    for tap_row in range(3):
        for tap_col in range(3):
            window = padded[:, tap_row:tap_row + height, tap_col:tap_col + length].astype(jnp.float32)
            total = total + jnp.einsum('oi,irc->orc', weight[:, 3 * tap_row + tap_col, :].astype(jnp.float32), window)
    return total

def conv_back(padded, weight):
    height = padded.shape[1] - 2
    length = padded.shape[2] - 2
    total = jnp.zeros((weight.shape[2], height, length), jnp.float32)
    for tap_row in range(3):
        for tap_col in range(3):
            window = padded[:, 2 - tap_row:2 - tap_row + height, 2 - tap_col:2 - tap_col + length].astype(jnp.float32)
            total = total + jnp.einsum('oi,orc->irc', weight[:, 3 * tap_row + tap_col, :].astype(jnp.float32), window)
    return total

def weight_grad(upstream, padded):
    height = upstream.shape[1]
    length = upstream.shape[2]
    pieces = []
    for tap_row in range(3):
        for tap_col in range(3):
            window = padded[:, tap_row:tap_row + height, tap_col:tap_col + length].astype(jnp.float32)
            pieces.append(jnp.einsum('orc,irc->oi', upstream.astype(jnp.float32), window))
    return jnp.stack(pieces, axis=1)

def smooth_gelu(values):
    return jax.nn.gelu(values, approximate=True)

def resample(extended):
    lower = jnp.pad(extended, ((0, 0), (0, 1), (0, 0)))
    top_left = lower[:, :-1, :-1]
    top_right = lower[:, :-1, 1:]
    low_left = lower[:, 1:, :-1]
    low_right = lower[:, 1:, 1:]
    even_even = smooth_gelu(top_left)
    even_odd = smooth_gelu((top_left + top_right) * 0.5)
    odd_even = smooth_gelu((top_left + low_left) * 0.5)
    odd_odd = smooth_gelu((top_left + top_right + low_left + low_right) * 0.25)
    row_even = (even_odd[:, :, :-1] + 2.0 * even_even[:, :, 1:] + even_odd[:, :, 1:]) * 0.25
    row_odd = (odd_odd[:, :, :-1] + 2.0 * odd_even[:, :, 1:] + odd_odd[:, :, 1:]) * 0.25
    shifted = jnp.pad(row_odd, ((0, 0), (1, 0), (0, 0)))[:, :-1]
    return (shifted + 2.0 * row_even + row_odd) * 0.25

def periodic_resample(hidden_values):
    return resample(wrap_cols(hidden_values, 1))

def reference(field, first_weight, second_weight, cotangent):
    grad_scale = 1.0 / math.sqrt(ROWS * COLS)
    field_pad = pad_rows(wrap_cols(field, 1))
    hidden = conv_forward(field_pad, first_weight).astype(jnp.bfloat16)
    smooth_values, pullback = jax.vjp(periodic_resample, hidden.astype(jnp.float32))
    smooth = smooth_values.astype(jnp.bfloat16)
    cot_pad = pad_rows(wrap_cols(cotangent, 1))
    smooth_grad = conv_back(cot_pad, second_weight).astype(jnp.bfloat16)
    hidden_grad = pullback(smooth_grad.astype(jnp.float32))[0].astype(jnp.bfloat16)
    smooth_pad = pad_rows(wrap_cols(smooth, 1))
    second_grad = weight_grad(cotangent, smooth_pad) * grad_scale
    first_grad = weight_grad(hidden_grad, field_pad) * grad_scale
    hidden_pad = pad_rows(wrap_cols(hidden_grad, 1))
    field_grad = (cotangent.astype(jnp.float32) + conv_back(hidden_pad, first_weight)).astype(jnp.bfloat16)
    return (field_grad, first_grad, second_grad)
```

```python
import functools
import math

import jax
import jax.numpy as jnp
from jax import lax
from jax.experimental import pallas as pl
from jax.experimental.pallas import tpu as pltpu
from jax.sharding import PartitionSpec as P

EDGE = 8
SENT = 4
SHARES = 4
GELU_RATE = math.sqrt(2.0 / math.pi)
GELU_CUBE = 0.044715
PARAMS = pltpu.CompilerParams(vmem_limit_bytes=12 * 1024 * 1024)
F32 = jnp.float32
BF16 = jnp.bfloat16


def swap_pairs(count, distance):
    return [(i, i ^ distance) for i in range(count)]


def shift(values, by):
    if by == 0:
        return values
    return pltpu.roll(values, by % values.shape[0], 0)


def matmul(left, right):
    return lax.dot_general(left, right, (((1,), (0,)), ((), ())), preferred_element_type=F32)


def matmul_nt(left, right):
    return lax.dot_general(left, right, (((1,), (1,)), ((), ())), preferred_element_type=F32)


def gelu_pair(values):
    square = values * values
    bent = jnp.tanh(GELU_RATE * (values + GELU_CUBE * (square * values)))
    inner_slope = GELU_RATE * (1.0 + 3.0 * GELU_CUBE * square)
    lifted = 0.5 * (1.0 + bent)
    return values * lifted, lifted + 0.5 * values * (1.0 - bent * bent) * inner_slope


def fill_block(scratch, lane, body, low, high):
    rows, length, width = body.shape
    lanes = pl.ds(lane, width)
    unused = jnp.zeros((rows, EDGE - SENT, width), F32)
    scratch[1 : rows + 1, EDGE : EDGE + length, lanes] = body
    low = jnp.concatenate([unused, low.astype(F32)], axis=1).astype(BF16)
    scratch[1 : rows + 1, 0:EDGE, lanes] = low
    high = jnp.concatenate([high.astype(F32), unused], axis=1).astype(BF16)
    scratch[1 : rows + 1, EDGE + length :, lanes] = high


def clear_rows(scratch):
    scratch[0] = jnp.zeros(scratch.shape[1:], scratch.dtype)
    scratch[scratch.shape[0] - 1] = jnp.zeros(scratch.shape[1:], scratch.dtype)


def chan_lanes(width):
    mine = lax.axis_index("chan")
    own = pl.multiple_of(mine * width, width)
    other = pl.multiple_of((1 - mine) * width, width)
    return own, other


def prepare_kernel(
    field, cot, weight,
    packed, field_out, cot_out, flat_out, last_out, first_out, weight_own,
    raw, wide, sems,
):
    width, rows, length = field.shape
    part = width // SHARES
    pieces = rows * length // part
    lane_own, lane_oth = chan_lanes(width)
    start = pl.multiple_of(lax.axis_index("space") % SHARES * part, part)
    away = weight.at[:, pl.ds(start, part), pl.ds(lane_oth, width)]
    copies = [
        pltpu.make_async_copy(field, raw.at[0], sems.at[0]),
        pltpu.make_async_copy(cot, raw.at[1], sems.at[1]),
        pltpu.make_async_copy(away, packed.at[pl.ds(pieces, 9)], sems.at[2]),
        pltpu.make_async_copy(weight.at[:, :, pl.ds(lane_own, width)], weight_own, sems.at[3]),
    ]
    for copy in copies:
        copy.start()
    for number, target in enumerate((field_out, cot_out)):
        copies[number].wait()
        wide[...] = raw[number].astype(F32).reshape(width * rows, length)
        for r in range(rows):
            row = wide[pl.ds(r, width, stride=rows), :]
            turned = row.T
            last_out[number, r] = turned[length - SENT :].astype(BF16)
            first_out[number, r] = turned[:SENT].astype(BF16)
            turned = turned.astype(BF16)
            target[r] = turned
            if number == 0:
                step = length // part
                packed[r * step : (r + 1) * step] = turned.reshape(step, part, width)
            else:
                flat_out[:, r * length : (r + 1) * length] = row.astype(BF16)
    copies[2].wait()
    copies[3].wait()


def forward_kernel(
    scale, own, packed, both, sides, weight, cot_flat,
    slopes_out, right_out, smooth_out, sums_out, block, hidden,
):
    rows, length, width = own.shape
    wide = length + 2 * EDGE
    lane_own, lane_oth = chan_lanes(width)
    clear_rows(block)
    other = packed[: packed.shape[0] - 9].reshape(own.shape)
    fill_block(block, lane_own, own[...], both[0, 0], both[1, 0])
    fill_block(block, lane_oth, other, sides[0, 0], sides[1, 0])
    clear_rows(right_out)
    right_out[1 : rows + 1, :, pl.ds(lane_own, width)] = own[...]
    right_out[1 : rows + 1, :, pl.ds(lane_oth, width)] = other
    total = None
    for p in range(3):
        taps = weight[3 * p : 3 * p + 3].reshape(3 * width, 2 * width)
        part = matmul_nt(block[p : p + rows].reshape(rows * wide, 2 * width), taps)
        total = part if total is None else total + part
    flat = (
        shift(total[:, :width], 1)
        + total[:, width : 2 * width]
        + shift(total[:, 2 * width :], -1)
    )
    hidden[...] = flat.astype(BF16).astype(F32).reshape(rows, wide, width)
    odd_before = jnp.zeros((wide, width), F32)
    for r in range(rows):
        here = hidden[r]
        pair = here + hidden[r + 1] if r + 1 < rows else here
        even_even, slopes_out[0, r] = gelu_pair(here)
        even_odd, slopes_out[1, r] = gelu_pair((here + shift(here, -1)) * 0.5)
        odd_even, slopes_out[2, r] = gelu_pair(pair * 0.5)
        odd_odd, slopes_out[3, r] = gelu_pair((pair + shift(pair, -1)) * 0.25)
        row_even = (shift(even_odd, 1) + 2.0 * even_even + even_odd) * 0.25
        row_odd = (shift(odd_odd, 1) + 2.0 * odd_even + odd_odd) * 0.25
        smooth = (odd_before + 2.0 * row_even + row_odd) * 0.25
        for q in range(3):
            moved = shift(smooth, 1 - q)[EDGE : EDGE + length].astype(BF16)
            for p in range(3):
                target = r + 1 - p
                if 0 <= target < rows:
                    lanes = slice((3 * p + q) * width, (3 * p + q + 1) * width)
                    smooth_out[target * length : (target + 1) * length, lanes] = moved
        odd_before = row_odd
    nothing = jnp.zeros((length, 3 * width), BF16)
    smooth_out[:length, : 3 * width] = nothing
    smooth_out[(rows - 1) * length :, 6 * width :] = nothing
    sums_out[...] = scale * matmul(cot_flat[...], smooth_out[...])


def weight_sums(scale, upstream, right, left, result, keep, send):
    rows, length, lanes = right.shape[0] - 2, right.shape[1], right.shape[2]
    width = left.shape[0] // 3
    for r in range(rows):
        row = upstream(r)
        for q in range(3):
            moved = shift(row, q - 1)[EDGE : EDGE + length].astype(BF16)
            left[q * width : (q + 1) * width, r * length : (r + 1) * length] = moved.T
    for p in range(3):
        result[...] = scale * matmul(left[...], right[p : p + rows].reshape(rows * length, lanes))
        for q in range(3):
            split_rows(result, q * width, width, slice(None), keep, send, 3 * p + q)


def split_rows(result, start, width, lanes, keep, send, place):
    upper = lax.axis_index("space") % 2
    half = width // 2
    first = pl.multiple_of(start + upper * half, half)
    second = pl.multiple_of(start + (1 - upper) * half, half)
    keep[place] = result[pl.ds(first, half), lanes]
    send[place] = result[pl.ds(second, half), lanes].astype(BF16)


def backward_kernel(
    scale, cot_own, cot_oth, both, sides, weight_own, weight_pair, weight_rest, slopes,
    right,
    grad_out, keep, send, block, left, result, grads, weight_oth,
):
    rows, length, width = cot_own.shape
    wide = length + 2 * EDGE
    clear_rows(block)
    fill_block(block, 0, cot_own[...], both[0, 1], both[1, 1])
    fill_block(block, width, cot_oth[...], sides[0, 1], sides[1, 1])
    part = width // SHARES
    share = lax.axis_index("space") % SHARES
    for source, number, distance in (
        (weight_pair, 0, 0), (weight_pair, 1, 2), (weight_rest, 0, 1), (weight_rest, 1, 3)
    ):
        start = pl.multiple_of((share ^ distance) * part, part)
        weight_oth[:, pl.ds(start, part)] = source[number]
    total = None
    for p in range(3):
        taps = jnp.concatenate(
            [
                jnp.concatenate([weight_own[3 * p + q] for q in range(3)], axis=1),
                jnp.concatenate([weight_oth[3 * p + q] for q in range(3)], axis=1),
            ],
            axis=0,
        )
        part = matmul(block[2 - p : 2 - p + rows].reshape(rows * wide, 2 * width), taps)
        total = part if total is None else total + part
    flat = (
        shift(total[:, :width], -1)
        + total[:, width : 2 * width]
        + shift(total[:, 2 * width :], 1)
    )
    grads[...] = flat.astype(BF16).astype(F32).reshape(rows, wide, width)
    odd_before = jnp.zeros((wide, width), F32)
    for r in range(rows):
        grad = grads[r]
        pair = grad + grads[r + 1] if r + 1 < rows else grad
        even_even = slopes[0, r] * grad * 0.25
        even_odd = slopes[1, r] * (grad + shift(grad, -1)) * 0.125
        odd_even = slopes[2, r] * pair * 0.125
        odd_odd = slopes[3, r] * (pair + shift(pair, -1)) * 0.0625
        row_even = even_even + 0.5 * (even_odd + shift(even_odd, 1))
        row_odd = 0.5 * odd_even + 0.25 * (odd_odd + shift(odd_odd, 1))
        rounded = (row_even + row_odd + odd_before).astype(BF16)
        grad_out[r] = rounded
        grads[r] = rounded.astype(F32)
        odd_before = row_odd
    weight_sums(scale, lambda r: grads[r], right, left, result, keep, send)


def second_kernel(scale, sums_own, cot_oth, smooth, keep, send, left, result):
    rows, length, width = cot_oth.shape
    for r in range(rows):
        left[:, r * length : (r + 1) * length] = cot_oth[r].T
    result[...] = scale * matmul(left[...], smooth[...])
    for side, sums in enumerate((sums_own, result)):
        for tap in range(9):
            lanes = slice(tap * width, (tap + 1) * width)
            split_rows(sums, 0, width, lanes, keep, send, 9 * side + tap)


def spread_kernel(grad, weight, keep, send, block, result):
    rows, wide, width = grad.shape
    length = wide - 2 * EDGE
    lane_own, lane_oth = chan_lanes(width)
    clear_rows(block)
    block[1 : rows + 1] = grad[...]
    columns = jnp.concatenate(
        [block[2 - p : 2 - p + rows].reshape(rows * wide, width) for p in range(3)], axis=1
    )
    total = None
    for q in range(3):
        taps = jnp.concatenate([weight[3 * p + q] for p in range(3)], axis=0)
        part = shift(matmul(columns, taps), q - 1)
        total = part if total is None else total + part
    result[...] = total.reshape(rows, wide, 2 * width)
    keep[...] = result[:, EDGE : EDGE + length, pl.ds(lane_own, width)]
    send[...] = result[:, EDGE : EDGE + length, pl.ds(lane_oth, width)].astype(BF16)


def run_kernel(kernel, outs, scratch, flops, *args, fetch=False):
    moved = sum(math.prod(shape) * jnp.dtype(kind).itemsize for shape, kind in outs)
    moved += sum(arg.size * arg.dtype.itemsize for arg in args)
    space = pltpu.HBM if fetch else pltpu.VMEM
    if fetch:
        args = [pltpu.with_memory_space_constraint(arg, pltpu.HBM) for arg in args]
    sems = [pltpu.SemaphoreType.DMA((4,))] if fetch else []
    return pl.pallas_call(
        kernel,
        cost_estimate=pl.CostEstimate(flops=flops, transcendentals=0, bytes_accessed=moved),
        out_shape=[jax.ShapeDtypeStruct(shape, kind) for shape, kind in outs],
        in_specs=[pl.BlockSpec(memory_space=space)] * len(args),
        out_specs=[pl.BlockSpec(memory_space=pltpu.VMEM)] * len(outs),
        scratch_shapes=[pltpu.VMEM(shape, kind) for shape, kind in scratch] + sems,
        compiler_params=PARAMS,
    )(*args)


def after(values, *others):
    return lax.optimization_barrier((values, *others))[0]


def split_half(values, upper):
    half = values.shape[1] // 2
    low, high = values[:, :half], values[:, half:]
    return jnp.where(upper, high, low), jnp.where(upper, low, high).astype(BF16)


def reduce_space(keep, send, count, steps, upper, others=None):
    sent = []
    for number, step in enumerate(steps[:-1]):
        sent.append(send)
        got = lax.ppermute(send, "space", swap_pairs(count, step))
        if others is not None:
            got = after(got, *others[number])
        values = keep + got.astype(F32)
        if number + 2 < len(steps):
            keep, send = split_half(values, upper[steps[number + 1]])
    mine = values.astype(BF16)
    sent.append(mine)
    got = lax.ppermute(mine, "space", swap_pairs(count, steps[-1]))
    if others is not None:
        got = after(got, *others[-1])
    return (mine.astype(F32) + got.astype(F32)).astype(BF16), sent


def gather_space(values, count, steps, upper):
    for step in reversed(steps[:-1]):
        got = lax.ppermute(values, "space", swap_pairs(count, step))
        values = jnp.concatenate(
            [
                jnp.where(upper[step], got, values),
                jnp.where(upper[step], values, got),
            ],
            axis=1,
        )
    return values.astype(F32).transpose(1, 0, 2)


def in_order(second, mine, theirs, axis):
    return jnp.concatenate(
        [jnp.where(second, theirs, mine), jnp.where(second, mine, theirs)], axis=axis
    )


def on_device(field, first_weight, second_weight, cotangent):
    width, rows, length = field.shape
    wide = length + 2 * EDGE
    count = lax.axis_size("space")
    scale = 1.0 / math.sqrt(rows * length * count)
    steps = [1 << b for b in range(count.bit_length() - 1)]
    bits = [(lax.axis_index("space") & step) != 0 for step in steps]
    field, second_part, *bits = lax.optimization_barrier(
        (field, lax.axis_index("chan") != 0, *bits)
    )
    upper = dict(zip(steps, bits))
    half = width // 2
    chan_swap = swap_pairs(2, 1)
    forward = [(i, (i + 1) % count) for i in range(count)]
    backward = [(target, source) for source, target in forward]

    block = (rows, length, width), BF16
    edge = (2, rows, SENT, width), BF16
    part = width // SHARES
    packed, field_own, cot_own, cot_flat, last, first, weight_own = run_kernel(
        prepare_kernel,
        [
            ((rows * length // part + 9, part, width), BF16),
            block, block, ((width, rows * length), BF16), edge, edge, ((9, width, width), BF16),
        ],
        [((2, width, rows, length), BF16), ((width * rows, length), F32)],
        0,
        field, cotangent, second_weight.transpose(1, 0, 2),
        fetch=True,
    )
    packed = lax.ppermute(packed, "chan", chan_swap)
    low = lax.ppermute(last, "space", forward)
    high = lax.ppermute(first, "space", backward)
    both = jnp.stack([low, high])
    sides = lax.ppermute(both, "chan", chan_swap)
    cot_oth = lax.ppermute(after(cot_own, low, high), "chan", chan_swap)
    weight_part = after(packed[-9:], sides)
    weight_next = lax.ppermute(weight_part, "space", swap_pairs(count, 2))
    first_taps = first_weight.transpose(1, 0, 2)

    conv_flops = 2 * rows * wide * 2 * width * 9 * width
    sums_flops = 2 * rows * length * 2 * width * 9 * width
    padded = (rows + 2, length, 2 * width), BF16
    slopes, field_rows, smooth, sums_own = run_kernel(
        functools.partial(forward_kernel, scale),
        [
            ((4, rows, wide, width), F32), padded,
            ((rows * length, 9 * width), BF16), ((width, 9 * width), F32),
        ],
        [((rows + 2, wide, 2 * width), BF16), ((rows, wide, width), F32)],
        2 * conv_flops + sums_flops // 2,
        field_own, packed, both, sides, first_taps, cot_flat,
    )
    weight_pair = jnp.stack([weight_part, after(weight_next, sums_own)])
    weight_rest = lax.ppermute(weight_pair, "space", swap_pairs(count, 1))
    second_keep, second_send = run_kernel(
        functools.partial(second_kernel, scale),
        [((18, half, width), F32), ((18, half, width), BF16)],
        [((width, rows * length), BF16), ((width, 9 * width), F32)],
        sums_flops // 2,
        sums_own, cot_oth, smooth,
    )
    hidden_grad, first_keep, first_send = run_kernel(
        functools.partial(backward_kernel, scale),
        [((rows, wide, width), BF16), ((9, half, 2 * width), F32), ((9, half, 2 * width), BF16)],
        [
            ((rows + 2, wide, 2 * width), BF16),
            ((3 * width, rows * length), BF16),
            ((3 * width, 2 * width), F32),
            ((rows, wide, width), F32),
            ((9, width, width), BF16),
        ],
        2 * conv_flops + sums_flops,
        cot_own, cot_oth, both, sides, weight_own, weight_pair, weight_rest, slopes, field_rows,
    )

    first_steps = steps[:1] + steps[2:-1] + steps[1:2] + steps[-1:] if count >= 8 else steps
    first_piece, sent = reduce_space(first_keep, first_send, count, first_steps, upper)

    field_keep, field_send = run_kernel(
        spread_kernel,
        [((rows, length, width), F32), ((rows, length, width), BF16)],
        [((rows + 2, wide, width), BF16), ((rows, wide, 2 * width), F32)],
        conv_flops,
        after(hidden_grad, sent[1]), first_taps,
    )
    field_got = lax.ppermute(field_send, "chan", chan_swap)
    field_sum = field_keep + after(field_got, sent[-1]).astype(F32)
    field_grad = (cot_own.astype(F32) + field_sum).astype(BF16).transpose(2, 0, 1)

    others = [(value,) for value in sent]
    others[1] += (field_send,)
    others[-1] += (field_grad,)
    second_piece, _ = reduce_space(second_keep, second_send, count, steps, upper, others)
    second_got = lax.ppermute(second_piece[9:], "chan", chan_swap)
    second_piece = in_order(second_part, second_piece[:9], second_got, 2)
    first_grad = gather_space(first_piece, count, first_steps, upper)
    second_grad = gather_space(second_piece, count, steps, upper)
    return (field_grad, first_grad, second_grad)


HALO = 3


def with_halo(block, width):
    count = lax.axis_size("space")
    forward = [(i, (i + 1) % count) for i in range(count)]
    backward = [(target, source) for source, target in forward]
    low = lax.ppermute(block[..., -width:], "space", forward)
    high = lax.ppermute(block[..., :width], "space", backward)
    return jnp.concatenate([low, block, high], axis=-1)


def pad_rows(values):
    return jnp.pad(values, ((0, 0), (1, 1), (0, 0)))


def collect(values):
    return lax.all_gather(values, "chan", axis=0, tiled=True)


def conv_forward(padded, weight):
    height = padded.shape[1] - 2
    length = padded.shape[2] - 2
    total = jnp.zeros((weight.shape[0], height, length), jnp.float32)
    for tap_row in range(3):
        for tap_col in range(3):
            window = padded[:, tap_row : tap_row + height, tap_col : tap_col + length]
            total = total + jnp.einsum(
                "oi,irc->orc",
                weight[:, 3 * tap_row + tap_col, :],
                window,
                preferred_element_type=jnp.float32,
            )
    return total


def conv_back(padded, weight):
    height = padded.shape[1] - 2
    length = padded.shape[2] - 2
    total = jnp.zeros((weight.shape[2], height, length), jnp.float32)
    for tap_row in range(3):
        for tap_col in range(3):
            window = padded[
                :, 2 - tap_row : 2 - tap_row + height, 2 - tap_col : 2 - tap_col + length
            ]
            total = total + jnp.einsum(
                "oi,orc->irc",
                weight[:, 3 * tap_row + tap_col, :],
                window,
                preferred_element_type=jnp.float32,
            )
    return total


def reduce_back(padded, weight):
    return lax.psum_scatter(conv_back(padded, weight), "chan", scatter_dimension=0, tiled=True)


def weight_grad(upstream, padded):
    height = upstream.shape[1]
    length = upstream.shape[2]
    pieces = []
    for tap_row in range(3):
        for tap_col in range(3):
            window = padded[:, tap_row : tap_row + height, tap_col : tap_col + length]
            pieces.append(
                jnp.einsum("orc,irc->oi", upstream, window, preferred_element_type=jnp.float32)
            )
    return jnp.stack(pieces, axis=0)


def smooth_gelu(values):
    return jax.nn.gelu(values, approximate=True)


def resample(extended):
    lower = jnp.pad(extended, ((0, 0), (0, 1), (0, 0)))
    top_left = lower[:, :-1, :-1]
    top_right = lower[:, :-1, 1:]
    low_left = lower[:, 1:, :-1]
    low_right = lower[:, 1:, 1:]
    even_even = smooth_gelu(top_left)
    even_odd = smooth_gelu((top_left + top_right) * 0.5)
    odd_even = smooth_gelu((top_left + low_left) * 0.5)
    odd_odd = smooth_gelu((top_left + top_right + low_left + low_right) * 0.25)
    row_even = (even_odd[:, :, :-1] + 2.0 * even_even[:, :, 1:] + even_odd[:, :, 1:]) * 0.25
    row_odd = (odd_odd[:, :, :-1] + 2.0 * odd_even[:, :, 1:] + odd_odd[:, :, 1:]) * 0.25
    shifted = jnp.pad(row_odd, ((0, 0), (1, 0), (0, 0)))[:, :-1]
    return (shifted + 2.0 * row_even + row_odd) * 0.25


def sum_over_space(values):
    count = lax.axis_size("space")
    place = lax.axis_index("space")
    steps = [1 << b for b in range(count.bit_length() - 1)]
    for step in steps:
        half = values.shape[1] // 2
        upper = (place & step) != 0
        low, high = values[:, :half], values[:, half:]
        sent = jnp.where(upper, low, high).astype(jnp.bfloat16)
        got = lax.ppermute(sent, "space", swap_pairs(count, step))
        values = jnp.where(upper, high, low) + got.astype(jnp.float32)
    values = values.astype(jnp.bfloat16)
    for step in reversed(steps):
        upper = (place & step) != 0
        got = lax.ppermute(values, "space", swap_pairs(count, step))
        values = jnp.concatenate(
            [jnp.where(upper, got, values), jnp.where(upper, values, got)], axis=1
        )
    return values.astype(jnp.float32).transpose(1, 0, 2)


def on_device_parts(field, first_weight, second_weight, cotangent):
    height = field.shape[1]
    length = field.shape[2]
    grad_scale = 1.0 / math.sqrt(height * length * lax.axis_size("space"))
    both = with_halo(jnp.concatenate([field, cotangent], axis=0), HALO)
    field_wide, cot_wide = jnp.split(both, 2, axis=0)
    field_all = collect(field_wide)
    field_pad = pad_rows(field_all)
    hidden = conv_forward(field_pad, first_weight).astype(jnp.bfloat16)
    smooth_sum = reduce_back(pad_rows(cot_wide), second_weight)
    smooth_grad = smooth_sum.astype(jnp.bfloat16)
    smooth = resample(hidden.astype(jnp.float32)).astype(jnp.bfloat16)
    smooth_all = collect(smooth)
    second_grad = weight_grad(cotangent, pad_rows(smooth_all)) * grad_scale
    wide_grad = smooth_grad.astype(jnp.float32)
    _, pull_wide = jax.vjp(
        resample, jnp.pad(hidden.astype(jnp.float32), ((0, 0), (0, 0), (1, 1)))
    )
    hidden_grad = pull_wide(wide_grad)[0][:, :, 2:-2].astype(jnp.bfloat16)
    first_grad = weight_grad(hidden_grad[:, :, 1:-1], field_pad[:, :, 2:-2]) * grad_scale
    field_sum = reduce_back(pad_rows(hidden_grad), first_weight)
    field_grad = (cotangent.astype(jnp.float32) + field_sum).astype(jnp.bfloat16)
    return (field_grad, sum_over_space(first_grad), sum_over_space(second_grad))


def solution(mesh):
    in_specs = (
        P("chan", None, "space"),
        P("chan", None, None),
        P("chan", None, None),
        P("chan", None, "space"),
    )
    out_specs = (P("chan", None, "space"), P("chan", None, None), P("chan", None, None))
    body = on_device if mesh.shape["chan"] == 2 else on_device_parts
    return jax.shard_map(
        body, mesh=mesh, in_specs=in_specs, out_specs=out_specs, check_vma=False
    )
```

```python
import functools
import math

import jax
import jax.numpy as jnp
from jax import lax
from jax.experimental import pallas as pl
from jax.experimental.pallas import tpu as pltpu
from jax.sharding import PartitionSpec as P

EDGE = 8
SENT = 4
SHARES = 4
GELU_RATE = math.sqrt(2.0 / math.pi)
GELU_CUBE = 0.044715
PARAMS = pltpu.CompilerParams(vmem_limit_bytes=12 * 1024 * 1024)
F32 = jnp.float32
BF16 = jnp.bfloat16


def swap_pairs(count, distance):
    return [(i, i ^ distance) for i in range(count)]


def shift(values, by):
    if by == 0:
        return values
    return pltpu.roll(values, by % values.shape[0], 0)


def matmul(left, right):
    return lax.dot_general(left, right, (((1,), (0,)), ((), ())), preferred_element_type=F32)


def matmul_nt(left, right):
    return lax.dot_general(left, right, (((1,), (1,)), ((), ())), preferred_element_type=F32)


def gelu_pair(values):
    square = values * values
    bent = jnp.tanh(GELU_RATE * (values + GELU_CUBE * (square * values)))
    inner_slope = GELU_RATE * (1.0 + 3.0 * GELU_CUBE * square)
    lifted = 0.5 * (1.0 + bent)
    return values * lifted, lifted + 0.5 * values * (1.0 - bent * bent) * inner_slope


def fill_block(scratch, lane, body, low, high):
    rows, length, width = body.shape
    lanes = pl.ds(lane, width)
    unused = jnp.zeros((rows, EDGE - SENT, width), F32)
    scratch[1 : rows + 1, EDGE : EDGE + length, lanes] = body
    low = jnp.concatenate([unused, low.astype(F32)], axis=1).astype(BF16)
    scratch[1 : rows + 1, 0:EDGE, lanes] = low
    high = jnp.concatenate([high.astype(F32), unused], axis=1).astype(BF16)
    scratch[1 : rows + 1, EDGE + length :, lanes] = high


def clear_rows(scratch):
    scratch[0] = jnp.zeros(scratch.shape[1:], scratch.dtype)
    scratch[scratch.shape[0] - 1] = jnp.zeros(scratch.shape[1:], scratch.dtype)


def chan_lanes(width):
    mine = lax.axis_index("chan")
    own = pl.multiple_of(mine * width, width)
    other = pl.multiple_of((1 - mine) * width, width)
    return own, other


def prepare_kernel(
    field, cot, weight,
    packed, field_out, cot_out, flat_out, last_out, first_out, weight_own,
    raw, wide, sems,
):
    width, rows, length = field.shape
    part = width // SHARES
    pieces = rows * length // part
    lane_own, lane_oth = chan_lanes(width)
    start = pl.multiple_of(lax.axis_index("space") % SHARES * part, part)
    away = weight.at[:, pl.ds(start, part), pl.ds(lane_oth, width)]
    copies = [
        pltpu.make_async_copy(field, raw.at[0], sems.at[0]),
        pltpu.make_async_copy(cot, raw.at[1], sems.at[1]),
        pltpu.make_async_copy(away, packed.at[pl.ds(pieces, 9)], sems.at[2]),
        pltpu.make_async_copy(weight.at[:, :, pl.ds(lane_own, width)], weight_own, sems.at[3]),
    ]
    for copy in copies:
        copy.start()
    for number, target in enumerate((field_out, cot_out)):
        copies[number].wait()
        wide[...] = raw[number].astype(F32).reshape(width * rows, length)
        for r in range(rows):
            row = wide[pl.ds(r, width, stride=rows), :]
            turned = row.T
            last_out[number, r] = turned[length - SENT :].astype(BF16)
            first_out[number, r] = turned[:SENT].astype(BF16)
            turned = turned.astype(BF16)
            target[r] = turned
            if number == 0:
                step = length // part
                packed[r * step : (r + 1) * step] = turned.reshape(step, part, width)
            else:
                flat_out[:, r * length : (r + 1) * length] = row.astype(BF16)
    copies[2].wait()
    copies[3].wait()


def forward_kernel(
    scale, own, packed, both, sides, weight, cot_flat,
    slopes_out, right_out, smooth_out, sums_out, block, hidden,
):
    rows, length, width = own.shape
    wide = length + 2 * EDGE
    lane_own, lane_oth = chan_lanes(width)
    clear_rows(block)
    other = packed[: packed.shape[0] - 9].reshape(own.shape)
    fill_block(block, lane_own, own[...], both[0, 0], both[1, 0])
    fill_block(block, lane_oth, other, sides[0, 0], sides[1, 0])
    clear_rows(right_out)
    right_out[1 : rows + 1, :, pl.ds(lane_own, width)] = own[...]
    right_out[1 : rows + 1, :, pl.ds(lane_oth, width)] = other
    total = None
    for p in range(3):
        taps = weight[3 * p : 3 * p + 3].reshape(3 * width, 2 * width)
        part = matmul_nt(block[p : p + rows].reshape(rows * wide, 2 * width), taps)
        total = part if total is None else total + part
    flat = (
        shift(total[:, :width], 1)
        + total[:, width : 2 * width]
        + shift(total[:, 2 * width :], -1)
    )
    hidden[...] = flat.astype(BF16).astype(F32).reshape(rows, wide, width)
    odd_before = jnp.zeros((wide, width), F32)
    for r in range(rows):
        here = hidden[r]
        pair = here + hidden[r + 1] if r + 1 < rows else here
        even_even, slopes_out[0, r] = gelu_pair(here)
        even_odd, slopes_out[1, r] = gelu_pair((here + shift(here, -1)) * 0.5)
        odd_even, slopes_out[2, r] = gelu_pair(pair * 0.5)
        odd_odd, slopes_out[3, r] = gelu_pair((pair + shift(pair, -1)) * 0.25)
        row_even = (shift(even_odd, 1) + 2.0 * even_even + even_odd) * 0.25
        row_odd = (shift(odd_odd, 1) + 2.0 * odd_even + odd_odd) * 0.25
        smooth = (odd_before + 2.0 * row_even + row_odd) * 0.25
        for q in range(3):
            moved = shift(smooth, 1 - q)[EDGE : EDGE + length].astype(BF16)
            for p in range(3):
                target = r + 1 - p
                if 0 <= target < rows:
                    lanes = slice((3 * p + q) * width, (3 * p + q + 1) * width)
                    smooth_out[target * length : (target + 1) * length, lanes] = moved
        odd_before = row_odd
    nothing = jnp.zeros((length, 3 * width), BF16)
    smooth_out[:length, : 3 * width] = nothing
    smooth_out[(rows - 1) * length :, 6 * width :] = nothing
    sums_out[...] = scale * matmul(cot_flat[...], smooth_out[...])


def weight_sums(scale, upstream, right, left, result, keep, send):
    rows, length, lanes = right.shape[0] - 2, right.shape[1], right.shape[2]
    width = left.shape[0] // 3
    for r in range(rows):
        row = upstream(r)
        for q in range(3):
            moved = shift(row, q - 1)[EDGE : EDGE + length].astype(BF16)
            left[q * width : (q + 1) * width, r * length : (r + 1) * length] = moved.T
    for p in range(3):
        result[...] = scale * matmul(left[...], right[p : p + rows].reshape(rows * length, lanes))
        for q in range(3):
            split_rows(result, q * width, width, slice(None), keep, send, 3 * p + q)


def split_rows(result, start, width, lanes, keep, send, place):
    upper = lax.axis_index("space") % 2
    half = width // 2
    first = pl.multiple_of(start + upper * half, half)
    second = pl.multiple_of(start + (1 - upper) * half, half)
    keep[place] = result[pl.ds(first, half), lanes]
    send[place] = result[pl.ds(second, half), lanes].astype(BF16)


def back_kernel(
    cot_own, cot_oth, both, sides, weight_own, weight_pair, weight_rest, grad_out, block, weight_oth
):
    rows, length, width = cot_own.shape
    wide = length + 2 * EDGE
    clear_rows(block)
    fill_block(block, 0, cot_own[...], both[0, 1], both[1, 1])
    fill_block(block, width, cot_oth[...], sides[0, 1], sides[1, 1])
    part = width // SHARES
    share = lax.axis_index("space") % SHARES
    for source, number, distance in (
        (weight_pair, 0, 0), (weight_pair, 1, 2), (weight_rest, 0, 1), (weight_rest, 1, 3)
    ):
        start = pl.multiple_of((share ^ distance) * part, part)
        weight_oth[:, pl.ds(start, part)] = source[number]
    total = None
    for p in range(3):
        taps = jnp.concatenate(
            [
                jnp.concatenate([weight_own[3 * p + q] for q in range(3)], axis=1),
                jnp.concatenate([weight_oth[3 * p + q] for q in range(3)], axis=1),
            ],
            axis=0,
        )
        part = matmul(block[2 - p : 2 - p + rows].reshape(rows * wide, 2 * width), taps)
        total = part if total is None else total + part
    flat = (
        shift(total[:, :width], -1)
        + total[:, width : 2 * width]
        + shift(total[:, 2 * width :], 1)
    )
    grad_out[...] = flat.astype(BF16).reshape(rows, wide, width)


def slope_kernel(scale, smooth_grad, slopes, right, grad_out, keep, send, left, result, grads):
    rows, wide, width = smooth_grad.shape
    odd_before = jnp.zeros((wide, width), F32)
    grad = smooth_grad[0].astype(F32)
    for r in range(rows):
        below = smooth_grad[r + 1].astype(F32) if r + 1 < rows else None
        pair = grad if below is None else grad + below
        even_even = slopes[0, r] * grad * 0.25
        even_odd = slopes[1, r] * (grad + shift(grad, -1)) * 0.125
        odd_even = slopes[2, r] * pair * 0.125
        odd_odd = slopes[3, r] * (pair + shift(pair, -1)) * 0.0625
        row_even = even_even + 0.5 * (even_odd + shift(even_odd, 1))
        row_odd = 0.5 * odd_even + 0.25 * (odd_odd + shift(odd_odd, 1))
        rounded = (row_even + row_odd + odd_before).astype(BF16)
        grad_out[r] = rounded
        grads[r] = rounded.astype(F32)
        odd_before = row_odd
        grad = below
    weight_sums(scale, lambda r: grads[r], right, left, result, keep, send)


def second_kernel(scale, sums_own, cot_oth, smooth, keep, send, left, result):
    rows, length, width = cot_oth.shape
    for r in range(rows):
        left[:, r * length : (r + 1) * length] = cot_oth[r].T
    result[...] = scale * matmul(left[...], smooth[...])
    for side, sums in enumerate((sums_own, result)):
        for tap in range(9):
            lanes = slice(tap * width, (tap + 1) * width)
            split_rows(sums, 0, width, lanes, keep, send, 9 * side + tap)


def spread_kernel(grad, weight, keep, send, block, result):
    rows, wide, width = grad.shape
    length = wide - 2 * EDGE
    lane_own, lane_oth = chan_lanes(width)
    clear_rows(block)
    block[1 : rows + 1] = grad[...]
    columns = jnp.concatenate(
        [block[2 - p : 2 - p + rows].reshape(rows * wide, width) for p in range(3)], axis=1
    )
    total = None
    for q in range(3):
        taps = jnp.concatenate([weight[3 * p + q] for p in range(3)], axis=0)
        part = shift(matmul(columns, taps), q - 1)
        total = part if total is None else total + part
    result[...] = total.reshape(rows, wide, 2 * width)
    keep[...] = result[:, EDGE : EDGE + length, pl.ds(lane_own, width)]
    send[...] = result[:, EDGE : EDGE + length, pl.ds(lane_oth, width)].astype(BF16)


def run_kernel(kernel, outs, scratch, flops, *args, fetch=False):
    moved = sum(math.prod(shape) * jnp.dtype(kind).itemsize for shape, kind in outs)
    moved += sum(arg.size * arg.dtype.itemsize for arg in args)
    space = pltpu.HBM if fetch else pltpu.VMEM
    if fetch:
        args = [pltpu.with_memory_space_constraint(arg, pltpu.HBM) for arg in args]
    sems = [pltpu.SemaphoreType.DMA((4,))] if fetch else []
    return pl.pallas_call(
        kernel,
        cost_estimate=pl.CostEstimate(flops=flops, transcendentals=0, bytes_accessed=moved),
        out_shape=[jax.ShapeDtypeStruct(shape, kind) for shape, kind in outs],
        in_specs=[pl.BlockSpec(memory_space=space)] * len(args),
        out_specs=[pl.BlockSpec(memory_space=pltpu.VMEM)] * len(outs),
        scratch_shapes=[pltpu.VMEM(shape, kind) for shape, kind in scratch] + sems,
        compiler_params=PARAMS,
    )(*args)


def after(values, *others):
    return lax.optimization_barrier((values, *others))[0]


def split_half(values, upper):
    half = values.shape[1] // 2
    low, high = values[:, :half], values[:, half:]
    return jnp.where(upper, high, low), jnp.where(upper, low, high).astype(BF16)


def reduce_space(keep, send, count, steps, upper, others=None):
    sent = []
    for number, step in enumerate(steps[:-1]):
        sent.append(send)
        got = lax.ppermute(send, "space", swap_pairs(count, step))
        if others is not None:
            got = after(got, *others[number])
        values = keep + got.astype(F32)
        if number + 2 < len(steps):
            keep, send = split_half(values, upper[steps[number + 1]])
    return values.astype(BF16), sent


def swap_pieces(piece, count, step, *others):
    got = after(lax.ppermute(piece, "space", swap_pairs(count, step)), *others)
    return (piece.astype(F32) + got.astype(F32)).astype(BF16)


def gather_space(values, count, steps, upper):
    for step in reversed(steps[:-1]):
        got = lax.ppermute(values, "space", swap_pairs(count, step))
        values = jnp.concatenate(
            [
                jnp.where(upper[step], got, values),
                jnp.where(upper[step], values, got),
            ],
            axis=1,
        )
    return values.astype(F32).transpose(1, 0, 2)


def in_order(second, mine, theirs, axis):
    return jnp.concatenate(
        [jnp.where(second, theirs, mine), jnp.where(second, mine, theirs)], axis=axis
    )


def on_device(field, first_weight, second_weight, cotangent):
    width, rows, length = field.shape
    wide = length + 2 * EDGE
    count = lax.axis_size("space")
    scale = 1.0 / math.sqrt(rows * length * count)
    steps = [1 << b for b in range(count.bit_length() - 1)]
    bits = [(lax.axis_index("space") & step) != 0 for step in steps]
    field, second_part, *bits = lax.optimization_barrier(
        (field, lax.axis_index("chan") != 0, *bits)
    )
    upper = dict(zip(steps, bits))
    half = width // 2
    chan_swap = swap_pairs(2, 1)
    forward = [(i, (i + 1) % count) for i in range(count)]
    backward = [(target, source) for source, target in forward]

    block = (rows, length, width), BF16
    edge = (2, rows, SENT, width), BF16
    part = width // SHARES
    packed, field_own, cot_own, cot_flat, last, first, weight_own = run_kernel(
        prepare_kernel,
        [
            ((rows * length // part + 9, part, width), BF16),
            block, block, ((width, rows * length), BF16), edge, edge, ((9, width, width), BF16),
        ],
        [((2, width, rows, length), BF16), ((width * rows, length), F32)],
        0,
        field, cotangent, second_weight.transpose(1, 0, 2),
        fetch=True,
    )
    packed = lax.ppermute(packed, "chan", chan_swap)
    low = lax.ppermute(last, "space", forward)
    high = lax.ppermute(first, "space", backward)
    both = jnp.stack([low, high])
    sides = lax.ppermute(both, "chan", chan_swap)
    cot_oth = lax.ppermute(after(cot_own, low, high), "chan", chan_swap)
    weight_part = after(packed[-9:], sides)
    weight_next = lax.ppermute(weight_part, "space", swap_pairs(count, 2))
    first_taps = first_weight.transpose(1, 0, 2)

    conv_flops = 2 * rows * wide * 2 * width * 9 * width
    sums_flops = 2 * rows * length * 2 * width * 9 * width
    padded = (rows + 2, length, 2 * width), BF16
    slopes, field_rows, smooth, sums_own = run_kernel(
        functools.partial(forward_kernel, scale),
        [
            ((4, rows, wide, width), F32), padded,
            ((rows * length, 9 * width), BF16), ((width, 9 * width), F32),
        ],
        [((rows + 2, wide, 2 * width), BF16), ((rows, wide, width), F32)],
        2 * conv_flops + sums_flops // 2,
        field_own, packed, both, sides, first_taps, cot_flat,
    )
    weight_pair = jnp.stack([weight_part, after(weight_next, sums_own)])
    weight_rest = lax.ppermute(weight_pair, "space", swap_pairs(count, 1))
    second_keep, second_send = run_kernel(
        functools.partial(second_kernel, scale),
        [((18, half, width), F32), ((18, half, width), BF16)],
        [((width, rows * length), BF16), ((width, 9 * width), F32)],
        sums_flops // 2,
        after(sums_own, weight_pair), cot_oth, smooth,
    )
    smooth_grad, = run_kernel(
        back_kernel,
        [((rows, wide, width), BF16)],
        [((rows + 2, wide, 2 * width), BF16), ((9, width, width), BF16)],
        3 * conv_flops,
        cot_own, cot_oth, both, sides, weight_own, weight_pair, weight_rest,
    )
    first_steps = steps[:1] + steps[2:-1] + steps[1:2] + steps[-1:] if count >= 8 else steps
    second_got = lax.ppermute(second_send, "space", swap_pairs(count, steps[0]))
    second_sum = second_keep + after(second_got, smooth_grad).astype(F32)
    second_keep, second_send = split_half(second_sum, upper[steps[1]])
    hidden_grad, first_keep, first_send = run_kernel(
        functools.partial(slope_kernel, scale),
        [((rows, wide, width), BF16), ((9, half, 2 * width), F32), ((9, half, 2 * width), BF16)],
        [
            ((3 * width, rows * length), BF16),
            ((3 * width, 2 * width), F32),
            ((rows, wide, width), F32),
        ],
        conv_flops + sums_flops,
        after(smooth_grad, second_send), slopes, field_rows,
    )
    first_piece, sent = reduce_space(first_keep, first_send, count, first_steps, upper)
    field_keep, field_send = run_kernel(
        spread_kernel,
        [((rows, length, width), F32), ((rows, length, width), BF16)],
        [((rows + 2, wide, width), BF16), ((rows, wide, 2 * width), F32)],
        0,
        hidden_grad, first_taps,
    )
    second_got = lax.ppermute(second_send, "space", swap_pairs(count, steps[1]))
    second_sum = second_keep + after(second_got, field_send).astype(F32)
    second_keep, second_send = split_half(second_sum, upper[steps[2]])

    field_got = lax.ppermute(field_send, "chan", chan_swap)
    field_sum = field_keep + after(field_got, first_piece).astype(F32)
    field_grad = (cot_own.astype(F32) + field_sum).astype(BF16).transpose(2, 0, 1)

    others = [(sent[2],)] + [(value,) for value in sent[2:]]
    second_piece, _ = reduce_space(second_keep, second_send, count, steps[2:], upper, others)
    second_piece = swap_pieces(second_piece, count, steps[-1], sent[-1])
    first_piece = swap_pieces(first_piece, count, steps[-1])
    second_got = after(lax.ppermute(second_piece[9:], "chan", chan_swap), field_grad)
    second_piece = in_order(second_part, second_piece[:9], second_got, 2)
    first_grad = gather_space(first_piece, count, first_steps, upper)
    second_grad = gather_space(second_piece, count, steps, upper)
    return (field_grad, first_grad, second_grad)


HALO = 3


def with_halo(block, width):
    count = lax.axis_size("space")
    forward = [(i, (i + 1) % count) for i in range(count)]
    backward = [(target, source) for source, target in forward]
    low = lax.ppermute(block[..., -width:], "space", forward)
    high = lax.ppermute(block[..., :width], "space", backward)
    return jnp.concatenate([low, block, high], axis=-1)


def pad_rows(values):
    return jnp.pad(values, ((0, 0), (1, 1), (0, 0)))


def collect(values):
    return lax.all_gather(values, "chan", axis=0, tiled=True)


def conv_forward(padded, weight):
    height = padded.shape[1] - 2
    length = padded.shape[2] - 2
    total = jnp.zeros((weight.shape[0], height, length), jnp.float32)
    for tap_row in range(3):
        for tap_col in range(3):
            window = padded[:, tap_row : tap_row + height, tap_col : tap_col + length]
            total = total + jnp.einsum(
                "oi,irc->orc",
                weight[:, 3 * tap_row + tap_col, :],
                window,
                preferred_element_type=jnp.float32,
            )
    return total


def conv_back(padded, weight):
    height = padded.shape[1] - 2
    length = padded.shape[2] - 2
    total = jnp.zeros((weight.shape[2], height, length), jnp.float32)
    for tap_row in range(3):
        for tap_col in range(3):
            window = padded[
                :, 2 - tap_row : 2 - tap_row + height, 2 - tap_col : 2 - tap_col + length
            ]
            total = total + jnp.einsum(
                "oi,orc->irc",
                weight[:, 3 * tap_row + tap_col, :],
                window,
                preferred_element_type=jnp.float32,
            )
    return total


def reduce_back(padded, weight):
    return lax.psum_scatter(conv_back(padded, weight), "chan", scatter_dimension=0, tiled=True)


def weight_grad(upstream, padded):
    height = upstream.shape[1]
    length = upstream.shape[2]
    pieces = []
    for tap_row in range(3):
        for tap_col in range(3):
            window = padded[:, tap_row : tap_row + height, tap_col : tap_col + length]
            pieces.append(
                jnp.einsum("orc,irc->oi", upstream, window, preferred_element_type=jnp.float32)
            )
    return jnp.stack(pieces, axis=0)


def smooth_gelu(values):
    return jax.nn.gelu(values, approximate=True)


def resample(extended):
    lower = jnp.pad(extended, ((0, 0), (0, 1), (0, 0)))
    top_left = lower[:, :-1, :-1]
    top_right = lower[:, :-1, 1:]
    low_left = lower[:, 1:, :-1]
    low_right = lower[:, 1:, 1:]
    even_even = smooth_gelu(top_left)
    even_odd = smooth_gelu((top_left + top_right) * 0.5)
    odd_even = smooth_gelu((top_left + low_left) * 0.5)
    odd_odd = smooth_gelu((top_left + top_right + low_left + low_right) * 0.25)
    row_even = (even_odd[:, :, :-1] + 2.0 * even_even[:, :, 1:] + even_odd[:, :, 1:]) * 0.25
    row_odd = (odd_odd[:, :, :-1] + 2.0 * odd_even[:, :, 1:] + odd_odd[:, :, 1:]) * 0.25
    shifted = jnp.pad(row_odd, ((0, 0), (1, 0), (0, 0)))[:, :-1]
    return (shifted + 2.0 * row_even + row_odd) * 0.25


def sum_over_space(values):
    count = lax.axis_size("space")
    place = lax.axis_index("space")
    steps = [1 << b for b in range(count.bit_length() - 1)]
    for step in steps:
        half = values.shape[1] // 2
        upper = (place & step) != 0
        low, high = values[:, :half], values[:, half:]
        sent = jnp.where(upper, low, high).astype(jnp.bfloat16)
        got = lax.ppermute(sent, "space", swap_pairs(count, step))
        values = jnp.where(upper, high, low) + got.astype(jnp.float32)
    values = values.astype(jnp.bfloat16)
    for step in reversed(steps):
        upper = (place & step) != 0
        got = lax.ppermute(values, "space", swap_pairs(count, step))
        values = jnp.concatenate(
            [jnp.where(upper, got, values), jnp.where(upper, values, got)], axis=1
        )
    return values.astype(jnp.float32).transpose(1, 0, 2)


def on_device_parts(field, first_weight, second_weight, cotangent):
    height = field.shape[1]
    length = field.shape[2]
    grad_scale = 1.0 / math.sqrt(height * length * lax.axis_size("space"))
    both = with_halo(jnp.concatenate([field, cotangent], axis=0), HALO)
    field_wide, cot_wide = jnp.split(both, 2, axis=0)
    field_all = collect(field_wide)
    field_pad = pad_rows(field_all)
    hidden = conv_forward(field_pad, first_weight).astype(jnp.bfloat16)
    smooth_sum = reduce_back(pad_rows(cot_wide), second_weight)
    smooth_grad = smooth_sum.astype(jnp.bfloat16)
    smooth = resample(hidden.astype(jnp.float32)).astype(jnp.bfloat16)
    smooth_all = collect(smooth)
    second_grad = weight_grad(cotangent, pad_rows(smooth_all)) * grad_scale
    wide_grad = smooth_grad.astype(jnp.float32)
    _, pull_wide = jax.vjp(
        resample, jnp.pad(hidden.astype(jnp.float32), ((0, 0), (0, 0), (1, 1)))
    )
    hidden_grad = pull_wide(wide_grad)[0][:, :, 2:-2].astype(jnp.bfloat16)
    first_grad = weight_grad(hidden_grad[:, :, 1:-1], field_pad[:, :, 2:-2]) * grad_scale
    field_sum = reduce_back(pad_rows(hidden_grad), first_weight)
    field_grad = (cotangent.astype(jnp.float32) + field_sum).astype(jnp.bfloat16)
    return (field_grad, sum_over_space(first_grad), sum_over_space(second_grad))


def solution(mesh):
    in_specs = (
        P("chan", None, "space"),
        P("chan", None, None),
        P("chan", None, None),
        P("chan", None, "space"),
    )
    out_specs = (P("chan", None, "space"), P("chan", None, None), P("chan", None, None))
    sizes = mesh.shape["chan"], mesh.shape["space"]
    body = on_device if sizes == (2, 16) else on_device_parts
    return jax.shard_map(
        body, mesh=mesh, in_specs=in_specs, out_specs=out_specs, check_vma=False
    )
```

```python
import functools
import math

import jax
import jax.numpy as jnp
from jax import lax
from jax.experimental import pallas as pl
from jax.experimental.pallas import tpu as pltpu
from jax.sharding import PartitionSpec as P

EDGE = 8
SENT = 4
SHARES = 4
GELU_RATE = math.sqrt(2.0 / math.pi)
GELU_CUBE = 0.044715
PARAMS = pltpu.CompilerParams(vmem_limit_bytes=12 * 1024 * 1024)
F32 = jnp.float32
BF16 = jnp.bfloat16


def swap_pairs(count, distance):
    return [(i, i ^ distance) for i in range(count)]


def shift(values, by):
    if by == 0:
        return values
    return pltpu.roll(values, by % values.shape[0], 0)


def matmul(left, right):
    return lax.dot_general(left, right, (((1,), (0,)), ((), ())), preferred_element_type=F32)


def matmul_nt(left, right):
    return lax.dot_general(left, right, (((1,), (1,)), ((), ())), preferred_element_type=F32)


def gelu_pair(values):
    square = values * values
    bent = jnp.tanh(GELU_RATE * (values + GELU_CUBE * (square * values)))
    inner_slope = GELU_RATE * (1.0 + 3.0 * GELU_CUBE * square)
    lifted = 0.5 * (1.0 + bent)
    return values * lifted, lifted + 0.5 * values * (1.0 - bent * bent) * inner_slope


def fill_block(scratch, lane, body, low, high):
    rows, length, width = body.shape
    lanes = pl.ds(lane, width)
    unused = jnp.zeros((rows, EDGE - SENT, width), F32)
    scratch[1 : rows + 1, EDGE : EDGE + length, lanes] = body
    low = jnp.concatenate([unused, low.astype(F32)], axis=1).astype(BF16)
    scratch[1 : rows + 1, 0:EDGE, lanes] = low
    high = jnp.concatenate([high.astype(F32), unused], axis=1).astype(BF16)
    scratch[1 : rows + 1, EDGE + length :, lanes] = high


def clear_rows(scratch):
    scratch[0] = jnp.zeros(scratch.shape[1:], scratch.dtype)
    scratch[scratch.shape[0] - 1] = jnp.zeros(scratch.shape[1:], scratch.dtype)


def chan_lanes(width):
    mine = lax.axis_index("chan")
    own = pl.multiple_of(mine * width, width)
    other = pl.multiple_of((1 - mine) * width, width)
    return own, other


def prepare_kernel(
    field, cot, weight,
    packed, field_out, cot_out, flat_out, last_out, first_out, weight_own,
    raw, wide, sems,
):
    width, rows, length = field.shape
    part = width // SHARES
    pieces = rows * length // part
    lane_own, lane_oth = chan_lanes(width)
    start = pl.multiple_of(lax.axis_index("space") % SHARES * part, part)
    away = weight.at[:, pl.ds(start, part), pl.ds(lane_oth, width)]
    copies = [
        pltpu.make_async_copy(field, raw.at[0], sems.at[0]),
        pltpu.make_async_copy(cot, raw.at[1], sems.at[1]),
        pltpu.make_async_copy(away, packed.at[pl.ds(pieces, 9)], sems.at[2]),
        pltpu.make_async_copy(weight.at[:, :, pl.ds(lane_own, width)], weight_own, sems.at[3]),
    ]
    for copy in copies:
        copy.start()
    for number, target in enumerate((field_out, cot_out)):
        copies[number].wait()
        wide[...] = raw[number].astype(F32).reshape(width * rows, length)
        for r in range(rows):
            row = wide[pl.ds(r, width, stride=rows), :]
            turned = row.T
            last_out[number, r] = turned[length - SENT :].astype(BF16)
            first_out[number, r] = turned[:SENT].astype(BF16)
            turned = turned.astype(BF16)
            target[r] = turned
            if number == 0:
                step = length // part
                packed[r * step : (r + 1) * step] = turned.reshape(step, part, width)
            else:
                flat_out[:, r * length : (r + 1) * length] = row.astype(BF16)
    copies[2].wait()
    copies[3].wait()


def forward_kernel(
    scale, own, packed, both, sides, weight, cot_flat,
    slopes_out, right_out, smooth_out, sums_out, block, hidden,
):
    rows, length, width = own.shape
    wide = length + 2 * EDGE
    lane_own, lane_oth = chan_lanes(width)
    clear_rows(block)
    other = packed[: packed.shape[0] - 9].reshape(own.shape)
    fill_block(block, lane_own, own[...], both[0, 0], both[1, 0])
    fill_block(block, lane_oth, other, sides[0, 0], sides[1, 0])
    clear_rows(right_out)
    right_out[1 : rows + 1, :, pl.ds(lane_own, width)] = own[...]
    right_out[1 : rows + 1, :, pl.ds(lane_oth, width)] = other
    total = None
    for p in range(3):
        taps = weight[3 * p : 3 * p + 3].reshape(3 * width, 2 * width)
        part = matmul_nt(block[p : p + rows].reshape(rows * wide, 2 * width), taps)
        total = part if total is None else total + part
    flat = (
        shift(total[:, :width], 1)
        + total[:, width : 2 * width]
        + shift(total[:, 2 * width :], -1)
    )
    hidden[...] = flat.astype(BF16).astype(F32).reshape(rows, wide, width)
    odd_before = jnp.zeros((wide, width), F32)
    for r in range(rows):
        here = hidden[r]
        pair = here + hidden[r + 1] if r + 1 < rows else here
        even_even, slopes_out[0, r] = gelu_pair(here)
        even_odd, slopes_out[1, r] = gelu_pair((here + shift(here, -1)) * 0.5)
        odd_even, slopes_out[2, r] = gelu_pair(pair * 0.5)
        odd_odd, slopes_out[3, r] = gelu_pair((pair + shift(pair, -1)) * 0.25)
        row_even = (shift(even_odd, 1) + 2.0 * even_even + even_odd) * 0.25
        row_odd = (shift(odd_odd, 1) + 2.0 * odd_even + odd_odd) * 0.25
        smooth = (odd_before + 2.0 * row_even + row_odd) * 0.25
        for q in range(3):
            moved = shift(smooth, 1 - q)[EDGE : EDGE + length].astype(BF16)
            for p in range(3):
                target = r + 1 - p
                if 0 <= target < rows:
                    lanes = slice((3 * p + q) * width, (3 * p + q + 1) * width)
                    smooth_out[target * length : (target + 1) * length, lanes] = moved
        odd_before = row_odd
    nothing = jnp.zeros((length, 3 * width), BF16)
    smooth_out[:length, : 3 * width] = nothing
    smooth_out[(rows - 1) * length :, 6 * width :] = nothing
    sums_out[...] = scale * matmul(cot_flat[...], smooth_out[...])


def weight_sums(scale, upstream, right, left, result, keep, send):
    rows, length, lanes = right.shape[0] - 2, right.shape[1], right.shape[2]
    width = left.shape[0] // 3
    for r in range(rows):
        row = upstream(r)
        for q in range(3):
            moved = shift(row, q - 1)[EDGE : EDGE + length].astype(BF16)
            left[q * width : (q + 1) * width, r * length : (r + 1) * length] = moved.T
    for p in range(3):
        result[...] = scale * matmul(left[...], right[p : p + rows].reshape(rows * length, lanes))
        for q in range(3):
            split_rows(result, q * width, width, slice(None), keep, send, 3 * p + q)


def split_rows(result, start, width, lanes, keep, send, place):
    upper = lax.axis_index("space") % 2
    half = width // 2
    first = pl.multiple_of(start + upper * half, half)
    second = pl.multiple_of(start + (1 - upper) * half, half)
    keep[place] = result[pl.ds(first, half), lanes]
    send[place] = result[pl.ds(second, half), lanes].astype(BF16)


def back_kernel(
    cot_own, cot_oth, both, sides, weight_own, weight_pair, weight_rest, grad_out, block, weight_oth
):
    rows, length, width = cot_own.shape
    wide = length + 2 * EDGE
    clear_rows(block)
    fill_block(block, 0, cot_own[...], both[0, 1], both[1, 1])
    fill_block(block, width, cot_oth[...], sides[0, 1], sides[1, 1])
    part = width // SHARES
    share = lax.axis_index("space") % SHARES
    for source, number, distance in (
        (weight_pair, 0, 0), (weight_pair, 1, 2), (weight_rest, 0, 1), (weight_rest, 1, 3)
    ):
        start = pl.multiple_of((share ^ distance) * part, part)
        weight_oth[:, pl.ds(start, part)] = source[number]
    total = None
    for p in range(3):
        taps = jnp.concatenate(
            [
                jnp.concatenate([weight_own[3 * p + q] for q in range(3)], axis=1),
                jnp.concatenate([weight_oth[3 * p + q] for q in range(3)], axis=1),
            ],
            axis=0,
        )
        part = matmul(block[2 - p : 2 - p + rows].reshape(rows * wide, 2 * width), taps)
        total = part if total is None else total + part
    flat = (
        shift(total[:, :width], -1)
        + total[:, width : 2 * width]
        + shift(total[:, 2 * width :], 1)
    )
    grad_out[...] = flat.astype(BF16).reshape(rows, wide, width)


def slope_kernel(scale, smooth_grad, slopes, right, grad_out, keep, send, left, result, grads):
    rows, wide, width = smooth_grad.shape
    odd_before = jnp.zeros((wide, width), F32)
    grad = smooth_grad[0].astype(F32)
    for r in range(rows):
        below = smooth_grad[r + 1].astype(F32) if r + 1 < rows else None
        pair = grad if below is None else grad + below
        even_even = slopes[0, r] * grad * 0.25
        even_odd = slopes[1, r] * (grad + shift(grad, -1)) * 0.125
        odd_even = slopes[2, r] * pair * 0.125
        odd_odd = slopes[3, r] * (pair + shift(pair, -1)) * 0.0625
        row_even = even_even + 0.5 * (even_odd + shift(even_odd, 1))
        row_odd = 0.5 * odd_even + 0.25 * (odd_odd + shift(odd_odd, 1))
        rounded = (row_even + row_odd + odd_before).astype(BF16)
        grad_out[r] = rounded
        grads[r] = rounded.astype(F32)
        odd_before = row_odd
        grad = below
    weight_sums(scale, lambda r: grads[r], right, left, result, keep, send)


def second_kernel(scale, sums_own, cot_oth, smooth, keep, send, left, result):
    rows, length, width = cot_oth.shape
    for r in range(rows):
        left[:, r * length : (r + 1) * length] = cot_oth[r].T
    result[...] = scale * matmul(left[...], smooth[...])
    for side, sums in enumerate((sums_own, result)):
        for tap in range(9):
            lanes = slice(tap * width, (tap + 1) * width)
            split_rows(sums, 0, width, lanes, keep, send, 9 * side + tap)


def spread_kernel(grad, weight, keep, send, block, result):
    rows, wide, width = grad.shape
    length = wide - 2 * EDGE
    lane_own, lane_oth = chan_lanes(width)
    clear_rows(block)
    block[1 : rows + 1] = grad[...]
    columns = jnp.concatenate(
        [block[2 - p : 2 - p + rows].reshape(rows * wide, width) for p in range(3)], axis=1
    )
    total = None
    for q in range(3):
        taps = jnp.concatenate([weight[3 * p + q] for p in range(3)], axis=0)
        part = shift(matmul(columns, taps), q - 1)
        total = part if total is None else total + part
    result[...] = total.reshape(rows, wide, 2 * width)
    keep[...] = result[:, EDGE : EDGE + length, pl.ds(lane_own, width)]
    send[...] = result[:, EDGE : EDGE + length, pl.ds(lane_oth, width)].astype(BF16)


def run_kernel(kernel, outs, scratch, flops, *args, fetch=False):
    moved = sum(math.prod(shape) * jnp.dtype(kind).itemsize for shape, kind in outs)
    moved += sum(arg.size * arg.dtype.itemsize for arg in args)
    space = pltpu.HBM if fetch else pltpu.VMEM
    if fetch:
        args = [pltpu.with_memory_space_constraint(arg, pltpu.HBM) for arg in args]
    sems = [pltpu.SemaphoreType.DMA((4,))] if fetch else []
    return pl.pallas_call(
        kernel,
        cost_estimate=pl.CostEstimate(flops=flops, transcendentals=0, bytes_accessed=moved),
        out_shape=[jax.ShapeDtypeStruct(shape, kind) for shape, kind in outs],
        in_specs=[pl.BlockSpec(memory_space=space)] * len(args),
        out_specs=[pl.BlockSpec(memory_space=pltpu.VMEM)] * len(outs),
        scratch_shapes=[pltpu.VMEM(shape, kind) for shape, kind in scratch] + sems,
        compiler_params=PARAMS,
    )(*args)


def after(values, *others):
    return lax.optimization_barrier((values, *others))[0]


def split_half(values, upper):
    half = values.shape[1] // 2
    low, high = values[:, :half], values[:, half:]
    return jnp.where(upper, high, low), jnp.where(upper, low, high).astype(BF16)


def reduce_space(keep, send, count, steps, upper, others=None):
    sent = []
    for number, step in enumerate(steps[:-1]):
        sent.append(send)
        got = lax.ppermute(send, "space", swap_pairs(count, step))
        if others is not None:
            got = after(got, *others[number])
        values = keep + got.astype(F32)
        if number + 2 < len(steps):
            keep, send = split_half(values, upper[steps[number + 1]])
    return values.astype(BF16), sent


def swap_pieces(piece, count, step, *others):
    got = after(lax.ppermute(piece, "space", swap_pairs(count, step)), *others)
    return (piece.astype(F32) + got.astype(F32)).astype(BF16)


def gather_space(values, count, steps, upper):
    for step in reversed(steps[:-1]):
        got = lax.ppermute(values, "space", swap_pairs(count, step))
        values = jnp.concatenate(
            [
                jnp.where(upper[step], got, values),
                jnp.where(upper[step], values, got),
            ],
            axis=1,
        )
    return values.astype(F32).transpose(1, 0, 2)


def in_order(second, mine, theirs, axis):
    return jnp.concatenate(
        [jnp.where(second, theirs, mine), jnp.where(second, mine, theirs)], axis=axis
    )


def on_device(field, first_weight, second_weight, cotangent):
    width, rows, length = field.shape
    wide = length + 2 * EDGE
    count = lax.axis_size("space")
    scale = 1.0 / math.sqrt(rows * length * count)
    steps = [1 << b for b in range(count.bit_length() - 1)]
    bits = [(lax.axis_index("space") & step) != 0 for step in steps]
    field, second_part, *bits = lax.optimization_barrier(
        (field, lax.axis_index("chan") != 0, *bits)
    )
    upper = dict(zip(steps, bits))
    half = width // 2
    chan_swap = swap_pairs(2, 1)
    forward = [(i, (i + 1) % count) for i in range(count)]
    backward = [(target, source) for source, target in forward]

    block = (rows, length, width), BF16
    edge = (2, rows, SENT, width), BF16
    part = width // SHARES
    packed, field_own, cot_own, cot_flat, last, first, weight_own = run_kernel(
        prepare_kernel,
        [
            ((rows * length // part + 9, part, width), BF16),
            block, block, ((width, rows * length), BF16), edge, edge, ((9, width, width), BF16),
        ],
        [((2, width, rows, length), BF16), ((width * rows, length), F32)],
        0,
        field, cotangent, second_weight.transpose(1, 0, 2),
        fetch=True,
    )
    packed = lax.ppermute(packed, "chan", chan_swap)
    low = lax.ppermute(last, "space", forward)
    high = lax.ppermute(first, "space", backward)
    both = jnp.stack([low, high])
    sides = lax.ppermute(both, "chan", chan_swap)
    cot_oth = lax.ppermute(after(cot_own, low, high), "chan", chan_swap)
    weight_part = after(packed[-9:], sides)
    weight_next = lax.ppermute(weight_part, "space", swap_pairs(count, 2))
    first_taps = first_weight.transpose(1, 0, 2)

    conv_flops = 2 * rows * wide * 2 * width * 9 * width
    sums_flops = 2 * rows * length * 2 * width * 9 * width
    padded = (rows + 2, length, 2 * width), BF16
    slopes, field_rows, smooth, sums_own = run_kernel(
        functools.partial(forward_kernel, scale),
        [
            ((4, rows, wide, width), F32), padded,
            ((rows * length, 9 * width), BF16), ((width, 9 * width), F32),
        ],
        [((rows + 2, wide, 2 * width), BF16), ((rows, wide, width), F32)],
        2 * conv_flops + sums_flops // 2,
        field_own, packed, both, sides, first_taps, cot_flat,
    )
    weight_pair = jnp.stack([weight_part, after(weight_next, sums_own)])
    weight_rest = lax.ppermute(weight_pair, "space", swap_pairs(count, 1))
    second_keep, second_send = run_kernel(
        functools.partial(second_kernel, scale),
        [((18, half, width), F32), ((18, half, width), BF16)],
        [((width, rows * length), BF16), ((width, 9 * width), F32)],
        sums_flops // 2,
        after(sums_own, weight_pair), cot_oth, smooth,
    )
    smooth_grad, = run_kernel(
        back_kernel,
        [((rows, wide, width), BF16)],
        [((rows + 2, wide, 2 * width), BF16), ((9, width, width), BF16)],
        3 * conv_flops,
        cot_own, cot_oth, both, sides, weight_own, weight_pair, weight_rest,
    )
    second_got = lax.ppermute(second_send, "space", swap_pairs(count, steps[0]))
    second_sum = second_keep + after(second_got, smooth_grad).astype(F32)
    second_keep, second_send = split_half(second_sum, upper[steps[1]])
    hidden_grad, first_keep, first_send = run_kernel(
        functools.partial(slope_kernel, scale),
        [((rows, wide, width), BF16), ((9, half, 2 * width), F32), ((9, half, 2 * width), BF16)],
        [
            ((3 * width, rows * length), BF16),
            ((3 * width, 2 * width), F32),
            ((rows, wide, width), F32),
        ],
        conv_flops + sums_flops,
        after(smooth_grad, second_send), slopes, field_rows,
    )
    first_piece, sent = reduce_space(first_keep, first_send, count, steps, upper)

    field_keep, field_send = run_kernel(
        spread_kernel,
        [((rows, length, width), F32), ((rows, length, width), BF16)],
        [((rows + 2, wide, width), BF16), ((rows, wide, 2 * width), F32)],
        conv_flops,
        after(hidden_grad, sent[1]), first_taps,
    )
    field_got = lax.ppermute(field_send, "chan", chan_swap)
    field_sum = field_keep + after(field_got, first_piece).astype(F32)
    field_grad = (cot_own.astype(F32) + field_sum).astype(BF16).transpose(2, 0, 1)

    others = [(sent[0],), (sent[1], field_send)] + [(value,) for value in sent[2:]]
    second_piece, _ = reduce_space(second_keep, second_send, count, steps[1:], upper, others)
    second_piece = swap_pieces(second_piece, count, steps[-1], sent[-1])
    first_piece = swap_pieces(first_piece, count, steps[-1])
    second_got = after(lax.ppermute(second_piece[9:], "chan", chan_swap), field_grad)
    second_piece = in_order(second_part, second_piece[:9], second_got, 2)
    first_grad = gather_space(first_piece, count, steps, upper)
    second_grad = gather_space(second_piece, count, steps, upper)
    return (field_grad, first_grad, second_grad)


HALO = 3


def with_halo(block, width):
    count = lax.axis_size("space")
    forward = [(i, (i + 1) % count) for i in range(count)]
    backward = [(target, source) for source, target in forward]
    low = lax.ppermute(block[..., -width:], "space", forward)
    high = lax.ppermute(block[..., :width], "space", backward)
    return jnp.concatenate([low, block, high], axis=-1)


def pad_rows(values):
    return jnp.pad(values, ((0, 0), (1, 1), (0, 0)))


def collect(values):
    return lax.all_gather(values, "chan", axis=0, tiled=True)


def conv_forward(padded, weight):
    height = padded.shape[1] - 2
    length = padded.shape[2] - 2
    total = jnp.zeros((weight.shape[0], height, length), jnp.float32)
    for tap_row in range(3):
        for tap_col in range(3):
            window = padded[:, tap_row : tap_row + height, tap_col : tap_col + length]
            total = total + jnp.einsum(
                "oi,irc->orc",
                weight[:, 3 * tap_row + tap_col, :],
                window,
                preferred_element_type=jnp.float32,
            )
    return total


def conv_back(padded, weight):
    height = padded.shape[1] - 2
    length = padded.shape[2] - 2
    total = jnp.zeros((weight.shape[2], height, length), jnp.float32)
    for tap_row in range(3):
        for tap_col in range(3):
            window = padded[
                :, 2 - tap_row : 2 - tap_row + height, 2 - tap_col : 2 - tap_col + length
            ]
            total = total + jnp.einsum(
                "oi,orc->irc",
                weight[:, 3 * tap_row + tap_col, :],
                window,
                preferred_element_type=jnp.float32,
            )
    return total


def reduce_back(padded, weight):
    return lax.psum_scatter(conv_back(padded, weight), "chan", scatter_dimension=0, tiled=True)


def weight_grad(upstream, padded):
    height = upstream.shape[1]
    length = upstream.shape[2]
    pieces = []
    for tap_row in range(3):
        for tap_col in range(3):
            window = padded[:, tap_row : tap_row + height, tap_col : tap_col + length]
            pieces.append(
                jnp.einsum("orc,irc->oi", upstream, window, preferred_element_type=jnp.float32)
            )
    return jnp.stack(pieces, axis=0)


def smooth_gelu(values):
    return jax.nn.gelu(values, approximate=True)


def resample(extended):
    lower = jnp.pad(extended, ((0, 0), (0, 1), (0, 0)))
    top_left = lower[:, :-1, :-1]
    top_right = lower[:, :-1, 1:]
    low_left = lower[:, 1:, :-1]
    low_right = lower[:, 1:, 1:]
    even_even = smooth_gelu(top_left)
    even_odd = smooth_gelu((top_left + top_right) * 0.5)
    odd_even = smooth_gelu((top_left + low_left) * 0.5)
    odd_odd = smooth_gelu((top_left + top_right + low_left + low_right) * 0.25)
    row_even = (even_odd[:, :, :-1] + 2.0 * even_even[:, :, 1:] + even_odd[:, :, 1:]) * 0.25
    row_odd = (odd_odd[:, :, :-1] + 2.0 * odd_even[:, :, 1:] + odd_odd[:, :, 1:]) * 0.25
    shifted = jnp.pad(row_odd, ((0, 0), (1, 0), (0, 0)))[:, :-1]
    return (shifted + 2.0 * row_even + row_odd) * 0.25


def sum_over_space(values):
    count = lax.axis_size("space")
    place = lax.axis_index("space")
    steps = [1 << b for b in range(count.bit_length() - 1)]
    for step in steps:
        half = values.shape[1] // 2
        upper = (place & step) != 0
        low, high = values[:, :half], values[:, half:]
        sent = jnp.where(upper, low, high).astype(jnp.bfloat16)
        got = lax.ppermute(sent, "space", swap_pairs(count, step))
        values = jnp.where(upper, high, low) + got.astype(jnp.float32)
    values = values.astype(jnp.bfloat16)
    for step in reversed(steps):
        upper = (place & step) != 0
        got = lax.ppermute(values, "space", swap_pairs(count, step))
        values = jnp.concatenate(
            [jnp.where(upper, got, values), jnp.where(upper, values, got)], axis=1
        )
    return values.astype(jnp.float32).transpose(1, 0, 2)


def on_device_parts(field, first_weight, second_weight, cotangent):
    height = field.shape[1]
    length = field.shape[2]
    grad_scale = 1.0 / math.sqrt(height * length * lax.axis_size("space"))
    both = with_halo(jnp.concatenate([field, cotangent], axis=0), HALO)
    field_wide, cot_wide = jnp.split(both, 2, axis=0)
    field_all = collect(field_wide)
    field_pad = pad_rows(field_all)
    hidden = conv_forward(field_pad, first_weight).astype(jnp.bfloat16)
    smooth_sum = reduce_back(pad_rows(cot_wide), second_weight)
    smooth_grad = smooth_sum.astype(jnp.bfloat16)
    smooth = resample(hidden.astype(jnp.float32)).astype(jnp.bfloat16)
    smooth_all = collect(smooth)
    second_grad = weight_grad(cotangent, pad_rows(smooth_all)) * grad_scale
    wide_grad = smooth_grad.astype(jnp.float32)
    _, pull_wide = jax.vjp(
        resample, jnp.pad(hidden.astype(jnp.float32), ((0, 0), (0, 0), (1, 1)))
    )
    hidden_grad = pull_wide(wide_grad)[0][:, :, 2:-2].astype(jnp.bfloat16)
    first_grad = weight_grad(hidden_grad[:, :, 1:-1], field_pad[:, :, 2:-2]) * grad_scale
    field_sum = reduce_back(pad_rows(hidden_grad), first_weight)
    field_grad = (cotangent.astype(jnp.float32) + field_sum).astype(jnp.bfloat16)
    return (field_grad, sum_over_space(first_grad), sum_over_space(second_grad))


def solution(mesh):
    in_specs = (
        P("chan", None, "space"),
        P("chan", None, None),
        P("chan", None, None),
        P("chan", None, "space"),
    )
    out_specs = (P("chan", None, "space"), P("chan", None, None), P("chan", None, None))
    sizes = mesh.shape["chan"], mesh.shape["space"]
    body = on_device if sizes == (2, 16) else on_device_parts
    return jax.shard_map(
        body, mesh=mesh, in_specs=in_specs, out_specs=out_specs, check_vma=False
    )
```

```python
import functools
import math

import jax
import jax.numpy as jnp
from jax import lax
from jax.experimental import pallas as pl
from jax.experimental.pallas import tpu as pltpu
from jax.sharding import PartitionSpec as P

EDGE = 8
SENT = 4
SHARES = 4
GELU_RATE = math.sqrt(2.0 / math.pi)
GELU_CUBE = 0.044715
PARAMS = pltpu.CompilerParams(vmem_limit_bytes=12 * 1024 * 1024)
F32 = jnp.float32
BF16 = jnp.bfloat16


def swap_pairs(count, distance):
    return [(i, i ^ distance) for i in range(count)]


def step_pairs(count, step):
    return [(i, i ^ step[i % 2]) for i in range(count)]


def shift(values, by):
    if by == 0:
        return values
    return pltpu.roll(values, by % values.shape[0], 0)


def matmul(left, right):
    return lax.dot_general(left, right, (((1,), (0,)), ((), ())), preferred_element_type=F32)


def matmul_nt(left, right):
    return lax.dot_general(left, right, (((1,), (1,)), ((), ())), preferred_element_type=F32)


def gelu_pair(values):
    square = values * values
    gate = 0.5 + 0.5 * jnp.tanh(values * (GELU_RATE + GELU_RATE * GELU_CUBE * square))
    result = values * gate
    rise = 2.0 * GELU_RATE + 6.0 * GELU_RATE * GELU_CUBE * square
    return result, gate + result * (1.0 - gate) * rise


def fill_block(scratch, lane, body, low, high):
    rows, length, width = body.shape
    lanes = pl.ds(lane, width)
    unused = jnp.zeros((rows, EDGE - SENT, width), F32)
    scratch[1 : rows + 1, EDGE : EDGE + length, lanes] = body
    low = jnp.concatenate([unused, low.astype(F32)], axis=1).astype(BF16)
    scratch[1 : rows + 1, 0:EDGE, lanes] = low
    high = jnp.concatenate([high.astype(F32), unused], axis=1).astype(BF16)
    scratch[1 : rows + 1, EDGE + length :, lanes] = high


def clear_rows(scratch):
    scratch[0] = jnp.zeros(scratch.shape[1:], scratch.dtype)
    scratch[scratch.shape[0] - 1] = jnp.zeros(scratch.shape[1:], scratch.dtype)


def chan_lanes(width):
    mine = lax.axis_index("chan")
    own = pl.multiple_of(mine * width, width)
    other = pl.multiple_of((1 - mine) * width, width)
    return own, other


def prepare_kernel(
    field, cot, weight,
    packed, field_out, cot_out, flat_out, last_out, first_out, weight_own,
    raw, wide, sems,
):
    width, rows, length = field.shape
    part = width // SHARES
    pieces = rows * length // part
    lane_own, lane_oth = chan_lanes(width)
    start = pl.multiple_of(lax.axis_index("space") % SHARES * part, part)
    away = weight.at[:, pl.ds(start, part), pl.ds(lane_oth, width)]
    copies = [
        pltpu.make_async_copy(field, raw.at[0], sems.at[0]),
        pltpu.make_async_copy(cot, raw.at[1], sems.at[1]),
        pltpu.make_async_copy(away, packed.at[pl.ds(pieces, 9)], sems.at[2]),
        pltpu.make_async_copy(weight.at[:, :, pl.ds(lane_own, width)], weight_own, sems.at[3]),
    ]
    for copy in copies:
        copy.start()
    for number, target in enumerate((field_out, cot_out)):
        copies[number].wait()
        wide[...] = raw[number].astype(F32).reshape(width * rows, length)
        for r in range(rows):
            row = wide[pl.ds(r, width, stride=rows), :]
            turned = row.T
            last_out[number, r] = turned[length - SENT :].astype(BF16)
            first_out[number, r] = turned[:SENT].astype(BF16)
            turned = turned.astype(BF16)
            target[r] = turned
            if number == 0:
                step = length // part
                packed[r * step : (r + 1) * step] = turned.reshape(step, part, width)
            else:
                flat_out[:, r * length : (r + 1) * length] = row.astype(BF16)
    copies[2].wait()
    copies[3].wait()


def forward_kernel(
    scale, own, packed, both, sides, weight, cot_flat,
    slopes_out, right_out, smooth_out, sums_out, block, hidden,
):
    rows, length, width = own.shape
    wide = length + 2 * EDGE
    lane_own, lane_oth = chan_lanes(width)
    clear_rows(block)
    other = packed[: packed.shape[0] - 9].reshape(own.shape)
    fill_block(block, lane_own, own[...], both[0, 0], both[1, 0])
    fill_block(block, lane_oth, other, sides[0, 0], sides[1, 0])
    clear_rows(right_out)
    right_out[1 : rows + 1, :, pl.ds(lane_own, width)] = own[...]
    right_out[1 : rows + 1, :, pl.ds(lane_oth, width)] = other
    total = None
    for p in range(3):
        taps = weight[3 * p : 3 * p + 3].reshape(3 * width, 2 * width)
        part = matmul_nt(block[p : p + rows].reshape(rows * wide, 2 * width), taps)
        total = part if total is None else total + part
    flat = (
        shift(total[:, :width], 1)
        + total[:, width : 2 * width]
        + shift(total[:, 2 * width :], -1)
    )
    hidden[...] = flat.astype(BF16).astype(F32).reshape(rows, wide, width)
    odd_before = jnp.zeros((wide, width), F32)
    for r in range(rows):
        here = hidden[r]
        pair = here + hidden[r + 1] if r + 1 < rows else here
        even_even, slopes_out[0, r] = gelu_pair(here)
        even_odd, slopes_out[1, r] = gelu_pair((here + shift(here, -1)) * 0.5)
        odd_even, slopes_out[2, r] = gelu_pair(pair * 0.5)
        odd_odd, slopes_out[3, r] = gelu_pair((pair + shift(pair, -1)) * 0.25)
        row_even = (shift(even_odd, 1) + 2.0 * even_even + even_odd) * 0.25
        row_odd = (shift(odd_odd, 1) + 2.0 * odd_even + odd_odd) * 0.25
        smooth = (odd_before + 2.0 * row_even + row_odd) * 0.25
        for q in range(3):
            moved = shift(smooth, 1 - q)[EDGE : EDGE + length].astype(BF16)
            for p in range(3):
                target = r + 1 - p
                if 0 <= target < rows:
                    lanes = slice((3 * p + q) * width, (3 * p + q + 1) * width)
                    smooth_out[target * length : (target + 1) * length, lanes] = moved
        odd_before = row_odd
    nothing = jnp.zeros((length, 3 * width), BF16)
    smooth_out[:length, : 3 * width] = nothing
    smooth_out[(rows - 1) * length :, 6 * width :] = nothing
    sums_out[...] = scale * matmul(cot_flat[...], smooth_out[...])


def weight_sums(scale, upstream, right, left, result, keep, send):
    rows, length, lanes = right.shape[0] - 2, right.shape[1], right.shape[2]
    width = left.shape[0] // 3
    for r in range(rows):
        row = upstream(r)
        for q in range(3):
            moved = shift(row, q - 1)[EDGE : EDGE + length].astype(BF16)
            left[q * width : (q + 1) * width, r * length : (r + 1) * length] = moved.T
    for p in range(3):
        result[...] = scale * matmul(left[...], right[p : p + rows].reshape(rows * length, lanes))
        for q in range(3):
            split_rows(result, q * width, width, slice(None), keep, send, 3 * p + q)


def split_rows(result, start, width, lanes, keep, send, place):
    upper = lax.axis_index("space") % 2
    half = width // 2
    first = pl.multiple_of(start + upper * half, half)
    second = pl.multiple_of(start + (1 - upper) * half, half)
    keep[place] = result[pl.ds(first, half), lanes]
    send[place] = result[pl.ds(second, half), lanes].astype(BF16)


def back_kernel(
    cot_own, cot_oth, both, sides, weight_own, weight_pair, weight_rest, grad_out, block, weight_oth
):
    rows, length, width = cot_own.shape
    wide = length + 2 * EDGE
    clear_rows(block)
    fill_block(block, 0, cot_own[...], both[0, 1], both[1, 1])
    fill_block(block, width, cot_oth[...], sides[0, 1], sides[1, 1])
    part = width // SHARES
    share = lax.axis_index("space") % SHARES
    for source, number, distance in (
        (weight_pair, 0, 0), (weight_pair, 1, 2), (weight_rest, 0, 1), (weight_rest, 1, 3)
    ):
        start = pl.multiple_of((share ^ distance) * part, part)
        weight_oth[:, pl.ds(start, part)] = source[number]
    total = None
    for p in range(3):
        taps = jnp.concatenate(
            [
                jnp.concatenate([weight_own[3 * p + q] for q in range(3)], axis=1),
                jnp.concatenate([weight_oth[3 * p + q] for q in range(3)], axis=1),
            ],
            axis=0,
        )
        part = matmul(block[2 - p : 2 - p + rows].reshape(rows * wide, 2 * width), taps)
        total = part if total is None else total + part
    flat = (
        shift(total[:, :width], -1)
        + total[:, width : 2 * width]
        + shift(total[:, 2 * width :], 1)
    )
    grad_out[...] = flat.astype(BF16).reshape(rows, wide, width)


def slope_kernel(scale, smooth_grad, slopes, right, grad_out, keep, send, left, result, grads):
    rows, wide, width = smooth_grad.shape
    odd_before = jnp.zeros((wide, width), F32)
    grad = smooth_grad[0].astype(F32)
    for r in range(rows):
        below = smooth_grad[r + 1].astype(F32) if r + 1 < rows else None
        pair = grad if below is None else grad + below
        even_even = slopes[0, r] * grad * 0.25
        even_odd = slopes[1, r] * (grad + shift(grad, -1)) * 0.125
        odd_even = slopes[2, r] * pair * 0.125
        odd_odd = slopes[3, r] * (pair + shift(pair, -1)) * 0.0625
        row_even = even_even + 0.5 * (even_odd + shift(even_odd, 1))
        row_odd = 0.5 * odd_even + 0.25 * (odd_odd + shift(odd_odd, 1))
        rounded = (row_even + row_odd + odd_before).astype(BF16)
        grad_out[r] = rounded
        grads[r] = rounded.astype(F32)
        odd_before = row_odd
        grad = below
    weight_sums(scale, lambda r: grads[r], right, left, result, keep, send)


def second_kernel(scale, sums_own, cot_oth, smooth, keep, send, left, result):
    rows, length, width = cot_oth.shape
    for r in range(rows):
        left[:, r * length : (r + 1) * length] = cot_oth[r].T
    result[...] = scale * matmul(left[...], smooth[...])
    for side, sums in enumerate((sums_own, result)):
        for tap in range(9):
            lanes = slice(tap * width, (tap + 1) * width)
            split_rows(sums, 0, width, lanes, keep, send, 9 * side + tap)


def spread_kernel(grad, weight, keep, send, block, result):
    rows, wide, width = grad.shape
    length = wide - 2 * EDGE
    lane_own, lane_oth = chan_lanes(width)
    clear_rows(block)
    block[1 : rows + 1] = grad[...]
    columns = jnp.concatenate(
        [block[2 - p : 2 - p + rows].reshape(rows * wide, width) for p in range(3)], axis=1
    )
    total = None
    for q in range(3):
        taps = jnp.concatenate([weight[3 * p + q] for p in range(3)], axis=0)
        part = shift(matmul(columns, taps), q - 1)
        total = part if total is None else total + part
    result[...] = total.reshape(rows, wide, 2 * width)
    keep[...] = result[:, EDGE : EDGE + length, pl.ds(lane_own, width)]
    send[...] = result[:, EDGE : EDGE + length, pl.ds(lane_oth, width)].astype(BF16)


def run_kernel(kernel, outs, scratch, flops, *args, fetch=False):
    moved = sum(math.prod(shape) * jnp.dtype(kind).itemsize for shape, kind in outs)
    moved += sum(arg.size * arg.dtype.itemsize for arg in args)
    space = pltpu.HBM if fetch else pltpu.VMEM
    if fetch:
        args = [pltpu.with_memory_space_constraint(arg, pltpu.HBM) for arg in args]
    sems = [pltpu.SemaphoreType.DMA((4,))] if fetch else []
    return pl.pallas_call(
        kernel,
        cost_estimate=pl.CostEstimate(flops=flops, transcendentals=0, bytes_accessed=moved),
        out_shape=[jax.ShapeDtypeStruct(shape, kind) for shape, kind in outs],
        in_specs=[pl.BlockSpec(memory_space=space)] * len(args),
        out_specs=[pl.BlockSpec(memory_space=pltpu.VMEM)] * len(outs),
        scratch_shapes=[pltpu.VMEM(shape, kind) for shape, kind in scratch] + sems,
        compiler_params=PARAMS,
    )(*args)


def after(values, *others):
    return lax.optimization_barrier((values, *others))[0]


def split_half(values, upper):
    half = values.shape[1] // 2
    low, high = values[:, :half], values[:, half:]
    return jnp.where(upper, high, low), jnp.where(upper, low, high).astype(BF16)


def reduce_space(keep, send, count, steps, upper, others=None):
    sent = []
    for number, step in enumerate(steps[:-1]):
        sent.append(send)
        got = lax.ppermute(send, "space", step_pairs(count, step))
        if others is not None:
            got = after(got, *others[number])
        values = keep + got.astype(F32)
        if number + 2 < len(steps):
            keep, send = split_half(values, upper[steps[number + 1]])
    return values.astype(BF16), sent


def swap_pieces(piece, count, step, *others):
    got = after(lax.ppermute(piece, "space", step_pairs(count, step)), *others)
    return (piece.astype(F32) + got.astype(F32)).astype(BF16)


def gather_space(values, count, steps, upper):
    for step in reversed(steps[:-1]):
        got = lax.ppermute(values, "space", step_pairs(count, step))
        values = jnp.concatenate(
            [
                jnp.where(upper[step], got, values),
                jnp.where(upper[step], values, got),
            ],
            axis=1,
        )
    return values.astype(F32).transpose(1, 0, 2)


def in_order(second, mine, theirs, axis):
    return jnp.concatenate(
        [jnp.where(second, theirs, mine), jnp.where(second, mine, theirs)], axis=axis
    )


def on_device(field, first_weight, second_weight, cotangent):
    width, rows, length = field.shape
    wide = length + 2 * EDGE
    count = lax.axis_size("space")
    scale = 1.0 / math.sqrt(rows * length * count)
    steps = [(1, 1), (2, 4), (4, 2), (8, 8)]
    place = lax.axis_index("space")
    odd = (place & 1) != 0
    bits = [
        (odd & ((place & second) != 0)) | (~odd & ((place & first) != 0))
        for first, second in steps[:-1]
    ]
    field, second_part, *bits = lax.optimization_barrier(
        (field, lax.axis_index("chan") != 0, *bits)
    )
    upper = dict(zip(steps, bits))
    half = width // 2
    chan_swap = swap_pairs(2, 1)
    forward = [(i, (i + 1) % count) for i in range(count)]
    backward = [(target, source) for source, target in forward]

    block = (rows, length, width), BF16
    edge = (2, rows, SENT, width), BF16
    part = width // SHARES
    packed, field_own, cot_own, cot_flat, last, first, weight_own = run_kernel(
        prepare_kernel,
        [
            ((rows * length // part + 9, part, width), BF16),
            block, block, ((width, rows * length), BF16), edge, edge, ((9, width, width), BF16),
        ],
        [((2, width, rows, length), BF16), ((width * rows, length), F32)],
        0,
        field, cotangent, second_weight.transpose(1, 0, 2),
        fetch=True,
    )
    packed = lax.ppermute(packed, "chan", chan_swap)
    low = lax.ppermute(last, "space", forward)
    high = lax.ppermute(first, "space", backward)
    both = jnp.stack([low, high])
    sides = lax.ppermute(both, "chan", chan_swap)
    cot_oth = lax.ppermute(after(cot_own, low, high), "chan", chan_swap)
    weight_part = after(packed[-9:], sides)
    weight_next = lax.ppermute(weight_part, "space", swap_pairs(count, 2))
    first_taps = first_weight.transpose(1, 0, 2)

    conv_flops = 2 * rows * wide * 2 * width * 9 * width
    sums_flops = 2 * rows * length * 2 * width * 9 * width
    padded = (rows + 2, length, 2 * width), BF16
    slopes, field_rows, smooth, sums_own = run_kernel(
        functools.partial(forward_kernel, scale),
        [
            ((4, rows, wide, width), F32), padded,
            ((rows * length, 9 * width), BF16), ((width, 9 * width), F32),
        ],
        [((rows + 2, wide, 2 * width), BF16), ((rows, wide, width), F32)],
        2 * conv_flops + sums_flops // 2,
        field_own, packed, both, sides, first_taps, cot_flat,
    )
    weight_pair = jnp.stack([weight_part, after(weight_next, sums_own)])
    weight_rest = lax.ppermute(weight_pair, "space", swap_pairs(count, 1))
    second_keep, second_send = run_kernel(
        functools.partial(second_kernel, scale),
        [((18, half, width), F32), ((18, half, width), BF16)],
        [((width, rows * length), BF16), ((width, 9 * width), F32)],
        sums_flops // 2,
        after(sums_own, weight_pair), cot_oth, smooth,
    )
    smooth_grad, = run_kernel(
        back_kernel,
        [((rows, wide, width), BF16)],
        [((rows + 2, wide, 2 * width), BF16), ((9, width, width), BF16)],
        3 * conv_flops,
        cot_own, cot_oth, both, sides, weight_own, weight_pair, weight_rest,
    )
    first_steps = [steps[0], steps[2], steps[1], steps[3]]
    second_got = lax.ppermute(second_send, "space", step_pairs(count, steps[0]))
    second_sum = second_keep + after(second_got, smooth_grad).astype(F32)
    second_keep, second_send = split_half(second_sum, upper[steps[1]])
    hidden_grad, first_keep, first_send = run_kernel(
        functools.partial(slope_kernel, scale),
        [((rows, wide, width), BF16), ((9, half, 2 * width), F32), ((9, half, 2 * width), BF16)],
        [
            ((3 * width, rows * length), BF16),
            ((3 * width, 2 * width), F32),
            ((rows, wide, width), F32),
        ],
        conv_flops + sums_flops,
        after(smooth_grad, second_send), slopes, field_rows,
    )
    first_piece, sent = reduce_space(first_keep, first_send, count, first_steps, upper)

    field_keep, field_send = run_kernel(
        spread_kernel,
        [((rows, length, width), F32), ((rows, length, width), BF16)],
        [((rows + 2, wide, width), BF16), ((rows, wide, 2 * width), F32)],
        conv_flops,
        after(hidden_grad, sent[1]), first_taps,
    )
    field_got = lax.ppermute(field_send, "chan", chan_swap)
    field_sum = field_keep + after(field_got, first_piece).astype(F32)
    field_grad = (cot_own.astype(F32) + field_sum).astype(BF16).transpose(2, 0, 1)

    others = [(sent[0],), (sent[1], field_send)] + [(value,) for value in sent[2:]]
    second_piece, _ = reduce_space(second_keep, second_send, count, steps[1:], upper, others)
    second_piece = swap_pieces(second_piece, count, steps[-1], sent[-1])
    first_piece = swap_pieces(first_piece, count, steps[-1])
    second_got = after(lax.ppermute(second_piece[9:], "chan", chan_swap), field_grad)
    second_piece = in_order(second_part, second_piece[:9], second_got, 2)
    first_grad = gather_space(first_piece, count, first_steps, upper)
    second_grad = gather_space(second_piece, count, steps, upper)
    return (field_grad, first_grad, second_grad)


HALO = 3


def with_halo(block, width):
    count = lax.axis_size("space")
    forward = [(i, (i + 1) % count) for i in range(count)]
    backward = [(target, source) for source, target in forward]
    low = lax.ppermute(block[..., -width:], "space", forward)
    high = lax.ppermute(block[..., :width], "space", backward)
    return jnp.concatenate([low, block, high], axis=-1)


def pad_rows(values):
    return jnp.pad(values, ((0, 0), (1, 1), (0, 0)))


def collect(values):
    return lax.all_gather(values, "chan", axis=0, tiled=True)


def conv_forward(padded, weight):
    height = padded.shape[1] - 2
    length = padded.shape[2] - 2
    total = jnp.zeros((weight.shape[0], height, length), jnp.float32)
    for tap_row in range(3):
        for tap_col in range(3):
            window = padded[:, tap_row : tap_row + height, tap_col : tap_col + length]
            total = total + jnp.einsum(
                "oi,irc->orc",
                weight[:, 3 * tap_row + tap_col, :],
                window,
                preferred_element_type=jnp.float32,
            )
    return total


def conv_back(padded, weight):
    height = padded.shape[1] - 2
    length = padded.shape[2] - 2
    total = jnp.zeros((weight.shape[2], height, length), jnp.float32)
    for tap_row in range(3):
        for tap_col in range(3):
            window = padded[
                :, 2 - tap_row : 2 - tap_row + height, 2 - tap_col : 2 - tap_col + length
            ]
            total = total + jnp.einsum(
                "oi,orc->irc",
                weight[:, 3 * tap_row + tap_col, :],
                window,
                preferred_element_type=jnp.float32,
            )
    return total


def reduce_back(padded, weight):
    return lax.psum_scatter(conv_back(padded, weight), "chan", scatter_dimension=0, tiled=True)


def weight_grad(upstream, padded):
    height = upstream.shape[1]
    length = upstream.shape[2]
    pieces = []
    for tap_row in range(3):
        for tap_col in range(3):
            window = padded[:, tap_row : tap_row + height, tap_col : tap_col + length]
            pieces.append(
                jnp.einsum("orc,irc->oi", upstream, window, preferred_element_type=jnp.float32)
            )
    return jnp.stack(pieces, axis=0)


def smooth_gelu(values):
    return jax.nn.gelu(values, approximate=True)


def resample(extended):
    lower = jnp.pad(extended, ((0, 0), (0, 1), (0, 0)))
    top_left = lower[:, :-1, :-1]
    top_right = lower[:, :-1, 1:]
    low_left = lower[:, 1:, :-1]
    low_right = lower[:, 1:, 1:]
    even_even = smooth_gelu(top_left)
    even_odd = smooth_gelu((top_left + top_right) * 0.5)
    odd_even = smooth_gelu((top_left + low_left) * 0.5)
    odd_odd = smooth_gelu((top_left + top_right + low_left + low_right) * 0.25)
    row_even = (even_odd[:, :, :-1] + 2.0 * even_even[:, :, 1:] + even_odd[:, :, 1:]) * 0.25
    row_odd = (odd_odd[:, :, :-1] + 2.0 * odd_even[:, :, 1:] + odd_odd[:, :, 1:]) * 0.25
    shifted = jnp.pad(row_odd, ((0, 0), (1, 0), (0, 0)))[:, :-1]
    return (shifted + 2.0 * row_even + row_odd) * 0.25


def sum_over_space(values):
    count = lax.axis_size("space")
    place = lax.axis_index("space")
    steps = [1 << b for b in range(count.bit_length() - 1)]
    for step in steps:
        half = values.shape[1] // 2
        upper = (place & step) != 0
        low, high = values[:, :half], values[:, half:]
        sent = jnp.where(upper, low, high).astype(jnp.bfloat16)
        got = lax.ppermute(sent, "space", swap_pairs(count, step))
        values = jnp.where(upper, high, low) + got.astype(jnp.float32)
    values = values.astype(jnp.bfloat16)
    for step in reversed(steps):
        upper = (place & step) != 0
        got = lax.ppermute(values, "space", swap_pairs(count, step))
        values = jnp.concatenate(
            [jnp.where(upper, got, values), jnp.where(upper, values, got)], axis=1
        )
    return values.astype(jnp.float32).transpose(1, 0, 2)


def on_device_parts(field, first_weight, second_weight, cotangent):
    height = field.shape[1]
    length = field.shape[2]
    grad_scale = 1.0 / math.sqrt(height * length * lax.axis_size("space"))
    both = with_halo(jnp.concatenate([field, cotangent], axis=0), HALO)
    field_wide, cot_wide = jnp.split(both, 2, axis=0)
    field_all = collect(field_wide)
    field_pad = pad_rows(field_all)
    hidden = conv_forward(field_pad, first_weight).astype(jnp.bfloat16)
    smooth_sum = reduce_back(pad_rows(cot_wide), second_weight)
    smooth_grad = smooth_sum.astype(jnp.bfloat16)
    smooth = resample(hidden.astype(jnp.float32)).astype(jnp.bfloat16)
    smooth_all = collect(smooth)
    second_grad = weight_grad(cotangent, pad_rows(smooth_all)) * grad_scale
    wide_grad = smooth_grad.astype(jnp.float32)
    _, pull_wide = jax.vjp(
        resample, jnp.pad(hidden.astype(jnp.float32), ((0, 0), (0, 0), (1, 1)))
    )
    hidden_grad = pull_wide(wide_grad)[0][:, :, 2:-2].astype(jnp.bfloat16)
    first_grad = weight_grad(hidden_grad[:, :, 1:-1], field_pad[:, :, 2:-2]) * grad_scale
    field_sum = reduce_back(pad_rows(hidden_grad), first_weight)
    field_grad = (cotangent.astype(jnp.float32) + field_sum).astype(jnp.bfloat16)
    return (field_grad, sum_over_space(first_grad), sum_over_space(second_grad))


def solution(mesh):
    in_specs = (
        P("chan", None, "space"),
        P("chan", None, None),
        P("chan", None, None),
        P("chan", None, "space"),
    )
    out_specs = (P("chan", None, "space"), P("chan", None, None), P("chan", None, None))
    sizes = mesh.shape["chan"], mesh.shape["space"]
    body = on_device if sizes == (2, 16) else on_device_parts
    return jax.shard_map(
        body, mesh=mesh, in_specs=in_specs, out_specs=out_specs, check_vma=False
    )
```
